128 devices in a mesh: replica: 8 (over x_lo, z), fsdp: 16 (over x_hi, y, core).
Axes of the slice: x: 4 (x_hi: 2, x_lo: 2; x = x_hi * 2 + x_lo), y: 4, z: 4, core: 2. Of those that a mesh axis runs over, the one named last changes fastest.
Arguments:
- local_params: float32 [8, 2048, 4096], P('replica', 'fsdp')
- params: float32 [2048, 4096], P('fsdp')
- momentum: float32 [2048, 4096], P('fsdp'), may hold values from -0.12 to 0.12
- old_mask: int32 [8], replicated, may hold values from 0 to 1, as said below
- attn: bfloat16 [8, 8192, 2048], P('replica', 'fsdp'), may hold values from -6 to 6
- resid: bfloat16 [8, 8192, 4096], P('replica', 'fsdp'), may hold values from -6 to 6
- gain: bfloat16 [4096], replicated, may hold values from 0.5 to 1.5
- out_grad: bfloat16 [8, 8192, 4096], P('replica', 'fsdp'), may hold values from -6 to 6
Outputs:
- new_params: float32 [2048, 4096], P('fsdp', 'replica')
- new_momentum: float32 [2048, 4096], P('fsdp', 'replica')
- weight_grad: bfloat16 [8, 2048, 4096], P('replica', 'fsdp')
- attn_grad: bfloat16 [8, 8192, 2048], P('replica', 'fsdp')
- resid_grad: bfloat16 [8, 8192, 4096], P('replica', 'fsdp')
The draws below stay inside these ranges and needn't reach their ends.
Inputs may be any that keep to these rules, and one draw needn't show every extreme that they name: `old_mask`: between 1 and 4 entries are 0, at drawn positions.
All inputs are finite; a program needn't handle non-finite values.
Results may differ from the reference program's by a relative error of at most 0.019.
Values may be sent and summed in bfloat16 or wider, within the bound.
A program may use at most 192 MiB of HBM per device.

```python
import math
import jax
import jax.numpy as jnp
from jax import lax

D = 4096
HQ = 2048
TOK_DEV = 512
TOKENS = 8192
REPLICAS = 8
N_FSDP = 16


def shared_params(key):
    return jax.random.normal(key, (HQ, D), jnp.float32) * HQ ** (-0.5)


def draw_params(key, part):
    return shared_params(key)


def draw_local_params(key, part):
    base = shared_params(key)
    key = jax.random.fold_in(key, 7)
    scale_key, common_key, noise_key = jax.random.split(key, 3)
    scales = 0.1 * jnp.exp(jax.random.uniform(scale_key, (REPLICAS, 1, 1), jnp.float32, 0.7, 1.6))
    position = jnp.arange(HQ, dtype=jnp.float32) / (HQ - 1)
    ramp = 1.0 + 2.0 * position
    common = jax.random.normal(common_key, (HQ, D), jnp.float32)
    noise = jax.random.normal(noise_key, (REPLICAS, HQ, D), jnp.float32)
    return base[None] - scales * ramp[None, :, None] * (common[None] + noise)


def draw_old_mask(key, part):
    key = jax.random.fold_in(key, 5)
    count_key, order_key = jax.random.split(key)
    joiners = jax.random.randint(count_key, (), 1, REPLICAS // 2 + 1)
    order = jax.random.permutation(order_key, REPLICAS)
    return (order >= joiners).astype(jnp.int32)


def level_of(own_key, dims, cuts, smallest, top_value):
    def one(axis_at, shards_of):
        draws = jax.random.uniform(jax.random.fold_in(jax.random.fold_in(own_key, 6), axis_at), (shards_of,), jnp.float32, smallest / len(cuts), top_value / len(cuts))
        return jnp.repeat(jnp.exp(draws), dims[axis_at] // shards_of).reshape((-1,) + (1,) * (len(dims) - axis_at - 1))

    loudness = one(*cuts[0])
    for cut in cuts[1:]:
        loudness = loudness * one(*cut)
    return loudness


def centred(own_key, dims, scale, most, shards=(), held_as=jnp.bfloat16):
    entries = jax.random.normal(own_key, dims, jnp.float32) * scale
    if len(shards) > 0:
        entries = level_of(own_key, dims, shards, -0.22, 0.18) * entries
    return jnp.clip(entries, min=-most, max=most).astype(held_as)


def setup_inputs(seed: int = 0) -> dict:
    seeds = jax.random.split(jax.random.key(seed), 9)
    local_params = draw_local_params(jax.random.fold_in(seeds[8], 71), 0)
    params = draw_params(jax.random.fold_in(seeds[8], 71), 0)
    momentum = centred(seeds[2], (HQ, D), 0.02, 0.12, ((0, 16),), jnp.float32)
    old_mask = draw_old_mask(jax.random.fold_in(seeds[8], 71), 0)
    attn = centred(seeds[4], (REPLICAS, TOKENS, HQ), 1.0, 6.0, ((0, 8), (1, 16)))
    resid = centred(seeds[5], (REPLICAS, TOKENS, D), 1.0, 6.0, ((0, 8), (1, 16)))
    gain = jnp.clip(1.0 + 0.1 * jax.random.normal(seeds[6], (D,), jnp.float32), 0.5, 1.5).astype(jnp.bfloat16)
    out_grad = centred(seeds[7], (REPLICAS, TOKENS, D), 1.0, 6.0, ((0, 8), (1, 16)))
    return {"local_params": local_params, "params": params, "momentum": momentum, "old_mask": old_mask, "attn": attn, "resid": resid, "gain": gain, "out_grad": out_grad}


outer_rate = 0.7
outer_beta = 0.9
clip_scale = 0.1

def inner_rows(weights, attn_r, resid_r, gain, out_r):
    hsum = resid_r.astype(jnp.float32) + jnp.dot(attn_r, weights, preferred_element_type=jnp.float32)
    inverse = lax.rsqrt(lax.optimization_barrier(jnp.mean(hsum * hsum, axis=-1, keepdims=True)) + 1e-05)
    scaled = out_r.astype(jnp.float32) * gain.astype(jnp.float32)
    project = lax.optimization_barrier(jnp.mean(scaled * hsum, axis=-1, keepdims=True))
    hgrad = (inverse * scaled - hsum * inverse ** 3 * project).astype(jnp.bfloat16)
    agrad = jnp.dot(hgrad, weights.T, preferred_element_type=jnp.float32).astype(jnp.bfloat16)
    return (hgrad, agrad)

def reference(local_params, params, momentum, old_mask, attn, resid, gain, out_grad):
    limit = clip_scale * math.sqrt(HQ * D)
    maskf = old_mask.astype(jnp.float32)
    total = jnp.zeros((HQ, D), jnp.float32)
    for replica in range(REPLICAS):
        delta = params - local_params[replica]
        norm_value = jnp.sqrt(jnp.sum(delta * delta))
        factor = jnp.minimum(jnp.float32(1.0), limit / (norm_value + 1e-06))
        total = total + maskf[replica] * factor * delta
    pseudo = total / jnp.sum(maskf)
    new_momentum = outer_beta * momentum + pseudo
    new_params = params - outer_rate * (pseudo + outer_beta * new_momentum)
    weights = new_params.astype(jnp.bfloat16)
    wgrads, agrads, hgrads = ([], [], [])
    for replica in range(REPLICAS):
        hgrad, agrad = inner_rows(weights, attn[replica], resid[replica], gain, out_grad[replica])
        blocks_a = attn[replica].reshape(N_FSDP, TOK_DEV, HQ)
        blocks_h = hgrad.reshape(N_FSDP, TOK_DEV, D)

        def add_block(carry, pair):
            part = lax.dot_general(pair[0], pair[1], (((0,), (0,)), ((), ())), preferred_element_type=jnp.float32)
            part = lax.optimization_barrier(part.astype(jnp.bfloat16))
            return (carry + part.astype(jnp.float32), None)
        summed, unused = lax.scan(add_block, jnp.zeros((HQ, D), jnp.float32), (blocks_a, blocks_h))
        wgrads.append(summed.astype(jnp.bfloat16))
        agrads.append(agrad)
        hgrads.append(hgrad)
    return (new_params, new_momentum, jnp.stack(wgrads), jnp.stack(agrads), jnp.stack(hgrads))
```

```python
import functools
import math

import jax
import jax.numpy as jnp
from jax import lax
from jax.experimental import pallas as pl
from jax.experimental.pallas import tpu as pltpu
from jax.sharding import PartitionSpec as P

D = 4096
HQ = 2048
TOK = 512

outer_rate = 0.7
outer_beta = 0.9
clip_scale = 0.1
BF16_MAX = float(jnp.finfo(jnp.bfloat16).max)

MESH = pl.DeviceIdType.MESH
BF = jnp.bfloat16
F32 = jnp.float32

PARTS = (
    (0, 96, 48, ("x", "y", "z")),
    (96, 80, 48, ("y", "z", "x")),
    (176, 80, 32, ("z", "x", "y")),
)
Y_UNITS = 5
X_UNITS = 3


def place():
    r = lax.axis_index("replica")
    f = lax.axis_index("fsdp")
    x = (f // 8) * 2 + r // 4
    return x, lax.rem(f // 2, 4), lax.rem(r, 4), lax.rem(f, 2)


def device(x, y, z, c):
    return (lax.rem(x, 2) * 4 + z, (x // 2) * 8 + y * 2 + c)


def up(i, n=4):
    return lax.rem(i + 1, n)


def down(i, n=4):
    return lax.rem(i + n - 1, n)


def remote(src, dst, send, recv, target):
    return pltpu.make_async_remote_copy(
        src_ref=src, dst_ref=dst, send_sem=send, recv_sem=recv, device_id=target, device_id_type=MESH
    )


def greet(targets):
    barrier = pltpu.get_barrier_semaphore()
    for target in targets:
        pl.semaphore_signal(barrier, inc=1, device_id=target, device_id_type=MESH)
    pl.semaphore_wait(barrier, len(targets))


def outer_kernel(
    lp, params, momentum, mask, attn, resid, gain, og,
    par_out, mom_out, w_out, hg_out, at_out,
    lv, pv, mv, dsend, drecv, nsend, nrecv, fsend, frecv, wb, w5, av, rv, ov, hs, hg, atv, stats, st_own, st_other,
    load_sem, mom_sem, d_send, d_recv, n_send, n_recv, f_send, f_recv, w_send, w_recv,
    act_own, act_send, act_recv, g_send, g_recv, s_send, s_recv, out_sem,
):
    x, y, z, c = place()
    r = lax.axis_index("replica")
    f = lax.axis_index("fsdp")
    other = 1 - c
    sibling = device(x, y, z, other)

    order = (4, 1, 2, 3, 5, 6, 7, 0)
    for k in order:
        cols = pl.ds(pl.multiple_of(lax.rem(r + k, 8) * 512, 512), 512)
        pltpu.make_async_copy(lp.at[:, cols], lv.at[k], load_sem.at[0, k]).start()
        pltpu.make_async_copy(params.at[:, cols], pv.at[k], load_sem.at[1, k]).start()
    own_cols = pl.ds(pl.multiple_of(r * 512, 512), 512)
    mom_copy = pltpu.make_async_copy(momentum.at[:, own_cols], mv, mom_sem)
    mom_copy.start()

    targets = [(lax.rem(r + k, 8), f) for k in range(1, 8)]
    targets += [(r, lax.rem(f + j, 16)) for j in range(1, 16)]
    outside = jnp.where(lax.rem(x, 2) == 0, down(x), up(x))
    targets.append(device(outside, y, z, c))
    greet(targets)

    squares = jnp.zeros((8, 512), F32)
    delta_copies = []
    for k in order:
        pltpu.make_async_copy(lv.at[k], lv.at[k], load_sem.at[0, k]).wait()
        pltpu.make_async_copy(pv.at[k], pv.at[k], load_sem.at[1, k]).wait()
        delta = pv[k] - lv[k]
        squares = squares + jnp.sum((delta * delta).reshape(16, 8, 512), axis=0)
        block = jnp.clip(delta, -BF16_MAX, BF16_MAX).astype(BF)
        if k == 0:
            drecv[0] = block
        else:
            dsend[k] = block
            copy = remote(
                dsend.at[k], drecv.at[k], d_send.at[k], d_recv.at[k], (lax.rem(r + k, 8), f)
            )
            copy.start()
            delta_copies.append(copy)

    tile = squares[:, 0:128] + squares[:, 128:256] + squares[:, 256:384] + squares[:, 384:512]
    nsend[...] = tile
    nrecv[0] = tile
    norm_copies = []
    for j in range(1, 16):
        copy = remote(nsend, nrecv.at[j], n_send.at[j], n_recv.at[j], (r, lax.rem(f + j, 16)))
        copy.start()
        norm_copies.append(copy)

    mine = pl.ds(pl.multiple_of(c * TOK, TOK), TOK)
    act_copies = []
    attn_own = pltpu.make_async_copy(attn, av.at[mine], act_own.at[0])
    attn_send = remote(attn, av.at[mine], act_send.at[0], act_recv.at[0], sibling)
    attn_own.start()
    attn_send.start()
    for k in range(8):
        for s, (src, dst) in enumerate(((resid, rv), (og, ov))):
            here = pl.ds(pl.multiple_of(k * 512 + c * 256, 256), 256)
            there = pl.ds(pl.multiple_of(k * 512 + other * 256, 256), 256)
            i = 1 + 2 * k + s
            a = pltpu.make_async_copy(src.at[:, here], dst.at[k, mine], act_own.at[i])
            b = remote(src.at[:, there], dst.at[k, mine], act_send.at[i], act_recv.at[i], sibling)
            a.start()
            b.start()
            act_copies.append((a, b))

    for copy in norm_copies:
        copy.wait_recv()
    total = jnp.full((8, 128), jnp.sum(nrecv[...]), F32)
    fsend[...] = total
    frecv[0] = total
    factor_copies = []
    for k in range(1, 8):
        copy = remote(fsend, frecv.at[k], f_send.at[k], f_recv.at[k], (lax.rem(r + k, 8), f))
        copy.start()
        factor_copies.append(copy)
    for copy in factor_copies:
        copy.wait_recv()
    limit = clip_scale * math.sqrt(HQ * D)
    factors = jnp.minimum(F32(1.0), limit / (jnp.sqrt(frecv[...]) + 1e-06))
    count = F32(0.0)
    for k in range(8):
        count = count + mask[k].astype(F32)

    pseudo = jnp.zeros((128, 512), F32)
    for copy in delta_copies:
        copy.wait_recv()
    for k in range(8):
        weight = mask[lax.rem(r + 8 - k, 8)].astype(F32) * jnp.max(factors[k])
        pseudo = pseudo + drecv[k].astype(F32) * weight
    pseudo = pseudo / count
    mom_copy.wait()
    new_mom = outer_beta * mv[...] + pseudo
    new_par = pv[0] - outer_rate * (pseudo + outer_beta * new_mom)
    mom_out[...] = new_mom
    par_out[...] = new_par
    rounded = new_par.astype(BF)
    wb[0] = rounded[:, 0:256]
    wb[1] = rounded[:, 256:512]

    rows = pl.ds(pl.multiple_of(c * 128, 128), 128)
    swap = remote(wb.at[other], w5.at[x, z, y, rows], w_send, w_recv, sibling)
    swap.start()
    w5[x, z, y, rows, :] = wb[c]
    swap.wait_recv()

    index = {"x": x, "y": y, "z": z}

    def region(part, gathered, axis, i, half):
        start, size, cut, _ = PARTS[part]
        if half == 0:
            size = cut
        elif half == 1:
            start, size = start + cut, size - cut
        at = {a: (slice(None) if a in gathered else index[a]) for a in "xyz"}
        at[axis] = i
        return w5.at[at["x"], at["z"], at["y"], pl.ds(start, size), :]

    gather_copies = []

    def send(phase, part, kind, ref, axis, i):
        place_there = dict(index)
        place_there[axis] = i
        sem = (phase * 3 + part) * 4 + kind
        copy = remote(
            ref, ref, g_send.at[sem], g_recv.at[sem],
            device(place_there["x"], place_there["y"], place_there["z"], c),
        )
        copy.start()
        gather_copies.append(copy)

    def arrived(phase, part, kind, ref):
        sem = (phase * 3 + part) * 4 + kind
        pltpu.make_async_copy(ref, ref, g_recv.at[sem]).wait()

    for phase in range(3):
        for part in range(3):
            axes = PARTS[part][3]
            axis, gathered = axes[phase], axes[:phase]
            i = index[axis]
            own = region(part, gathered, axis, i, None)
            send(phase, part, 0, own, axis, up(i))
            send(phase, part, 1, own, axis, down(i))
        if phase == 2:
            attn_own.wait()
            attn_send.wait_recv()

            @pl.loop(0, 32)
            def _(t):
                tok = pl.ds(pl.multiple_of(lax.rem(t, 4) * 256, 256), 256)
                col = pl.ds(pl.multiple_of((t // 4) * 256, 256), 256)
                atv[t // 4, :, tok] = av[tok, col].T

            at_copy = pltpu.make_async_copy(atv, at_out, out_sem.at[0])
            at_copy.start()
        for part in range(3):
            axes = PARTS[part][3]
            axis, gathered = axes[phase], axes[:phase]
            i = index[axis]
            left = region(part, gathered, axis, down(i), None)
            right = region(part, gathered, axis, up(i), None)
            arrived(phase, part, 0, left)
            send(phase, part, 2, region(part, gathered, axis, down(i), 0), axis, up(i))
            arrived(phase, part, 1, right)
            send(phase, part, 3, region(part, gathered, axis, up(i), 1), axis, down(i))
        for part in range(3):
            axes = PARTS[part][3]
            axis, gathered = axes[phase], axes[:phase]
            far = lax.rem(index[axis] + 2, 4)
            arrived(phase, part, 2, region(part, gathered, axis, far, 0))
            arrived(phase, part, 3, region(part, gathered, axis, far, 1))

    w_copy = pltpu.make_async_copy(w5, w_out, out_sem.at[1])
    w_copy.start()

    for a, b in act_copies:
        a.wait()
        b.wait_recv()
    stats[...] = jnp.zeros_like(stats)

    @pl.loop(0, 16)
    def _(t):
        k = t // 2
        tok = pl.ds(pl.multiple_of(lax.rem(t, 2) * 512, 512), 512)
        top = w5[k // 4, lax.rem(k, 4)].reshape(1024, 256)
        bottom = w5[k // 4 + 2, lax.rem(k, 4)].reshape(1024, 256)
        h = jnp.dot(av[tok, 0:1024], top, preferred_element_type=F32)
        h = h + jnp.dot(av[tok, 1024:2048], bottom, preferred_element_type=F32)
        h = h + rv[k, tok, :].astype(F32)
        hs[k, tok, :] = h
        sc = ov[k, tok, :].astype(F32) * gain[2 * k + c]
        hh = h * h
        sh = sc * h
        stats[0, tok, :] += hh[:, 0:128] + hh[:, 128:256]
        stats[1, tok, :] += sh[:, 0:128] + sh[:, 128:256]

    lane = lax.broadcasted_iota(jnp.int32, (256, 128), 1)

    @pl.loop(0, 4)
    def _(t):
        tok = pl.ds(pl.multiple_of(t * 256, 256), 256)
        a = jnp.sum(stats[0, tok, :], axis=1, keepdims=True)
        b = jnp.sum(stats[1, tok, :], axis=1, keepdims=True)
        st_own[tok, :] = jnp.where(lane < 64, a, b)

    st_copy = remote(st_own, st_other, s_send, s_recv, sibling)
    st_copy.start()
    st_copy.wait_recv()

    @pl.loop(0, 4)
    def _(t):
        tok = pl.ds(pl.multiple_of(t * 256, 256), 256)
        both = (st_own[tok, :] + st_other[tok, :]) * (1.0 / D)
        inv = lax.rsqrt(both[:, 0:1] + 1e-05)
        slope = inv * inv * inv * both[:, 64:65]
        for k in range(8):
            sc = ov[k, tok, :].astype(F32) * gain[2 * k + c]
            hg[k, tok, :] = (inv * sc - hs[k, tok, :] * slope).astype(BF)

    hg_copy = pltpu.make_async_copy(hg, hg_out, out_sem.at[2])
    hg_copy.start()

    for copy in delta_copies + norm_copies + factor_copies + gather_copies + [swap, st_copy, attn_send]:
        copy.wait_send()
    for _, b in act_copies:
        b.wait_send()
    at_copy.wait()
    w_copy.wait()
    hg_copy.wait()


def grad_kernel(
    at, hgr, w,
    wg_out, ag_out, hg_out,
    atv, hgv, w5, part, ry, ryx, rx, rxy, fin, agf, ags, agr,
    load_sem, y_send, y_recv, yx_send, yx_recv, x_send, x_recv, xy_send, xy_recv,
    fin_send, fin_recv, ag_send, ag_recv, hgo_own, hgo_send, hgo_recv,
):
    x, y, z, c = place()
    other = 1 - c
    xh = x // 2
    xo = 1 - xh
    sibling = device(x, y, z, other)
    yr, yl, yo = up(y), down(y), lax.rem(y + 2, 4)
    right, left = device(x, yr, z, c), device(x, yl, z, c)
    across = device(lax.rem(x + 2, 4), y, z, c)

    at_load = pltpu.make_async_copy(at, atv, load_sem.at[0])
    hg_load = pltpu.make_async_copy(hgr, hgv, load_sem.at[1])
    w_load = pltpu.make_async_copy(w, w5, load_sem.at[2])
    at_load.start()
    hg_load.start()
    w_load.start()
    greet([sibling, right, left, across])
    at_load.wait()
    hg_load.wait()

    def comp(k, h, d):
        acc = jnp.dot(atv[h * 4 + d], hgv[k], preferred_element_type=F32)
        part[k, h, d] = acc.astype(BF).reshape(2, 128, 256)

    def y_copy(u, m):
        d, h = ((yo, 0), (yo, 1), (yr, 1), (yl, 0), (yr, 0), (yl, 1))[m]
        target = right if m % 2 == 0 else left
        return remote(part.at[u, :, d, h], ry.at[u, m], y_send.at[u, m], y_recv.at[u, m], target)

    def yx_copy(u):
        return remote(part.at[u, xo, y], ryx.at[u], yx_send.at[u], yx_recv.at[u], across)

    def x_copy(v):
        return remote(part.at[Y_UNITS + v, xo], rx.at[v], x_send.at[v], x_recv.at[v], across)

    def xy_copy(v, m):
        d, h = ((yo, 0), (yo, 1), (yr, 1), (yl, 0), (yr, 0), (yl, 1))[m]
        target = right if m % 2 == 0 else left
        return remote(
            part.at[Y_UNITS + v, xh, d, h], rxy.at[v, m], xy_send.at[v, m], xy_recv.at[v, m], target
        )

    def x_start(v):
        for d in range(4):
            comp(Y_UNITS + v, xo, d)
        x_copy(v).start()

    def y_start(u):
        comp(u, 0, yo)
        comp(u, 1, yo)
        y_copy(u, 0).start()
        y_copy(u, 1).start()

    @pl.loop(0, X_UNITS)
    def _(v):
        x_start(v)
        y_start(v)

    @pl.loop(X_UNITS, Y_UNITS)
    def _(u):
        y_start(u)

    @pl.loop(0, Y_UNITS)
    def _(u):
        comp(u, 0, yr)
        comp(u, 1, yr)
        y_copy(u, 2).start()
        comp(u, 0, yl)
        comp(u, 1, yl)
        y_copy(u, 3).start()

    mine = pl.ds(pl.multiple_of(c * TOK, TOK), TOK)
    theirs = pl.ds(pl.multiple_of(other * TOK, TOK), TOK)

    def hgo_copies(k):
        cols = pl.ds(pl.multiple_of(k * 512 + c * 256, 256), 256)
        return (
            pltpu.make_async_copy(hgv.at[k, mine], hg_out.at[:, cols], hgo_own.at[k]),
            remote(hgv.at[k, theirs], hg_out.at[:, cols], hgo_send.at[k], hgo_recv.at[k], sibling),
        )

    @pl.loop(0, 8)
    def _(k):
        a, b = hgo_copies(k)
        a.start()
        b.start()

    @pl.loop(0, Y_UNITS)
    def _(u):
        comp(u, 0, y)
        comp(u, 1, y)

    @pl.loop(0, X_UNITS)
    def _(v):
        for d in range(4):
            comp(Y_UNITS + v, xh, d)

    def add(dst, src):
        part[dst] = (part[dst].astype(F32) + src.astype(F32)).astype(BF)

    @pl.loop(0, Y_UNITS)
    def _(u):
        y_copy(u, 0).wait_recv()
        for h in range(2):
            add((u, h, yr, 0), ry[u, 0, h])
        y_copy(u, 4).start()
        y_copy(u, 1).wait_recv()
        for h in range(2):
            add((u, h, yl, 1), ry[u, 1, h])
        y_copy(u, 5).start()

    def x_middle(v):
        x_copy(v).wait_recv()
        for d in (yo, yr, yl, y):
            for h in range(2):
                add((Y_UNITS + v, xh, d, h), rx[v, d, h])
            if d is yo:
                xy_copy(v, 0).start()
                xy_copy(v, 1).start()
        xy_copy(v, 2).start()
        xy_copy(v, 3).start()

    def y_finish(u):
        for m in (2, 3, 4, 5):
            y_copy(u, m).wait_recv()
        for h in range(2):
            for s, (m, n) in enumerate(((3, 4), (2, 5))):
                total = part[u, h, y, s].astype(F32) + ry[u, m, h].astype(F32) + ry[u, n, h].astype(F32)
                part[u, h, y, s] = total.astype(BF)
        yx_copy(u).start()

    x_middle(0)

    w_load.wait()

    def agrad(q, tok):
        wide = jnp.concatenate([w5[(q // 4) * 2 + k // 4, k % 4, lax.rem(q, 4)] for k in range(8)], axis=1)
        rows = jnp.concatenate([hgv[k, tok, :] for k in range(8)], axis=1)
        return lax.dot_general(rows, wide, (((1,), (1,)), ((), ())), preferred_element_type=F32)

    @pl.loop(0, 8)
    def _(q):
        ags[:, pl.ds(pl.multiple_of(q * 256, 256), 256)] = agrad(q, theirs).astype(BF)

    ag_copy = remote(ags, agr, ag_send, ag_recv, sibling)
    ag_copy.start()

    @pl.loop(0, 8)
    def _(q):
        agf[:, pl.ds(pl.multiple_of(q * 256, 256), 256)] = agrad(q, mine)

    ag_copy.wait_recv()

    @pl.loop(0, 8)
    def _(q):
        col = pl.ds(pl.multiple_of(q * 256, 256), 256)
        ag_out[:, col] = (agf[:, col] + agr[:, col].astype(F32)).astype(BF)

    x_middle(1)
    y_finish(0)
    x_middle(2)

    @pl.loop(1, Y_UNITS)
    def _(u):
        y_finish(u)

    @pl.loop(0, X_UNITS)
    def _(v):
        xy_copy(v, 0).wait_recv()
        add((Y_UNITS + v, xh, yr, 0), rxy[v, 0])
        xy_copy(v, 4).start()
        xy_copy(v, 1).wait_recv()
        add((Y_UNITS + v, xh, yl, 1), rxy[v, 1])
        xy_copy(v, 5).start()

    def fin_copy(k):
        cols = pl.ds(pl.multiple_of(k * 512 + c * 256, 256), 256)
        return remote(fin.at[k, other], wg_out.at[:, cols], fin_send.at[k], fin_recv.at[k], sibling)

    def deliver(k):
        fin_copy(k).start()
        cols = pl.ds(pl.multiple_of(k * 512 + c * 256, 256), 256)
        wg_out[:, cols] = fin[k, c]

    @pl.loop(0, Y_UNITS)
    def _(u):
        yx_copy(u).wait_recv()
        fin[u] = (part[u, xh, y].astype(F32) + ryx[u].astype(F32)).astype(BF)
        deliver(u)

    @pl.loop(0, X_UNITS)
    def _(v):
        for m in (2, 3, 4, 5):
            xy_copy(v, m).wait_recv()
        for s, (m, n) in enumerate(((3, 4), (2, 5))):
            total = part[Y_UNITS + v, xh, y, s].astype(F32) + rxy[v, m].astype(F32) + rxy[v, n].astype(F32)
            fin[Y_UNITS + v, s] = total.astype(BF)
        deliver(Y_UNITS + v)

    @pl.loop(0, 8)
    def _(k):
        copy = fin_copy(k)
        copy.wait_recv()
        copy.wait_send()
        a, b = hgo_copies(k)
        a.wait()
        b.wait_recv()
        b.wait_send()

    @pl.loop(0, Y_UNITS)
    def _(u):
        for m in range(6):
            y_copy(u, m).wait_send()
        yx_copy(u).wait_send()

    @pl.loop(0, X_UNITS)
    def _(v):
        x_copy(v).wait_send()
        for m in range(6):
            xy_copy(v, m).wait_send()

    ag_copy.wait_send()


def shards(local_params, params, momentum, old_mask, attn, resid, gain, out_grad):
    hbm = pl.BlockSpec(memory_space=pl.ANY)
    vmem = pl.BlockSpec(memory_space=pltpu.VMEM)
    smem = pl.BlockSpec(memory_space=pltpu.SMEM)
    dma = pltpu.SemaphoreType.DMA
    gains = gain.astype(F32).reshape(16, 1, 256)
    par, mom, w, hg, at = pl.pallas_call(
        outer_kernel,
        out_shape=(
            jax.ShapeDtypeStruct((128, 512), F32),
            jax.ShapeDtypeStruct((128, 512), F32),
            jax.ShapeDtypeStruct((4, 4, 4, 256, 256), BF),
            jax.ShapeDtypeStruct((8, 1024, 256), BF),
            jax.ShapeDtypeStruct((8, 256, 1024), BF),
        ),
        in_specs=[hbm, hbm, hbm, smem, hbm, hbm, vmem, hbm],
        out_specs=(vmem, vmem, hbm, hbm, hbm),
        scratch_shapes=[
            pltpu.VMEM((8, 128, 512), F32),
            pltpu.VMEM((8, 128, 512), F32),
            pltpu.VMEM((128, 512), F32),
            pltpu.VMEM((8, 128, 512), BF),
            pltpu.VMEM((8, 128, 512), BF),
            pltpu.VMEM((8, 128), F32),
            pltpu.VMEM((16, 8, 128), F32),
            pltpu.VMEM((8, 128), F32),
            pltpu.VMEM((8, 8, 128), F32),
            pltpu.VMEM((2, 128, 256), BF),
            pltpu.VMEM((4, 4, 4, 256, 256), BF),
            pltpu.VMEM((1024, 2048), BF),
            pltpu.VMEM((8, 1024, 256), BF),
            pltpu.VMEM((8, 1024, 256), BF),
            pltpu.VMEM((8, 1024, 256), F32),
            pltpu.VMEM((8, 1024, 256), BF),
            pltpu.VMEM((8, 256, 1024), BF),
            pltpu.VMEM((2, 1024, 128), F32),
            pltpu.VMEM((1024, 128), F32),
            pltpu.VMEM((1024, 128), F32),
            dma((2, 8)), dma, dma((8,)), dma((8,)), dma((16,)), dma((16,)), dma((8,)), dma((8,)), dma, dma,
            dma((17,)), dma((17,)), dma((17,)), dma((36,)), dma((36,)), dma, dma, dma((3,)),
        ],
        compiler_params=pltpu.CompilerParams(
            collective_id=0, has_side_effects=True, vmem_limit_bytes=56 << 20
        ),
        cost_estimate=pl.CostEstimate(flops=9 * 10**9, bytes_accessed=40 * 2**20, transcendentals=0),
        name="outer_step",
    )(local_params[0], params, momentum, old_mask, attn[0], resid[0], gains, out_grad[0])
    wg, ag, hgo = pl.pallas_call(
        grad_kernel,
        out_shape=(
            jax.ShapeDtypeStruct((128, D), BF),
            jax.ShapeDtypeStruct((TOK, HQ), BF),
            jax.ShapeDtypeStruct((TOK, D), BF),
        ),
        in_specs=[hbm, hbm, hbm],
        out_specs=(vmem, vmem, hbm),
        scratch_shapes=[
            pltpu.VMEM((8, 256, 1024), BF),
            pltpu.VMEM((8, 1024, 256), BF),
            pltpu.VMEM((4, 4, 4, 256, 256), BF),
            pltpu.VMEM((8, 2, 4, 2, 128, 256), BF),
            pltpu.VMEM((Y_UNITS, 6, 2, 128, 256), BF),
            pltpu.VMEM((Y_UNITS, 2, 128, 256), BF),
            pltpu.VMEM((X_UNITS, 4, 2, 128, 256), BF),
            pltpu.VMEM((X_UNITS, 6, 128, 256), BF),
            pltpu.VMEM((8, 2, 128, 256), BF),
            pltpu.VMEM((TOK, HQ), F32),
            pltpu.VMEM((TOK, HQ), BF),
            pltpu.VMEM((TOK, HQ), BF),
            dma((3,)), dma((Y_UNITS, 6)), dma((Y_UNITS, 6)), dma((Y_UNITS,)), dma((Y_UNITS,)),
            dma((X_UNITS,)), dma((X_UNITS,)), dma((X_UNITS, 6)), dma((X_UNITS, 6)),
            dma((8,)), dma((8,)), dma, dma, dma((8,)), dma((8,)), dma((8,)),
        ],
        compiler_params=pltpu.CompilerParams(
            collective_id=1, has_side_effects=True, vmem_limit_bytes=56 << 20
        ),
        cost_estimate=pl.CostEstimate(flops=18 * 10**9, bytes_accessed=40 * 2**20, transcendentals=0),
        name="inner_grads",
    )(at, hg, w)
    return (par, mom, wg[None], ag[None], hgo[None])


def solution(mesh):
    return jax.shard_map(
        shards,
        mesh=mesh,
        in_specs=(
            P("replica", "fsdp", None),
            P("fsdp", None),
            P("fsdp", None),
            P(),
            P("replica", "fsdp", None),
            P("replica", "fsdp", None),
            P(),
            P("replica", "fsdp", None),
        ),
        out_specs=(
            P("fsdp", "replica"),
            P("fsdp", "replica"),
            P("replica", "fsdp", None),
            P("replica", "fsdp", None),
            P("replica", "fsdp", None),
        ),
        check_vma=False,
    )
```

```python
import functools
import math

import jax
import jax.numpy as jnp
from jax import lax
from jax.experimental import pallas as pl
from jax.experimental.pallas import tpu as pltpu
from jax.sharding import PartitionSpec as P

D = 4096
HQ = 2048
TOK = 512

outer_rate = 0.7
outer_beta = 0.9
clip_scale = 0.1
BF16_MAX = float(jnp.finfo(jnp.bfloat16).max)

MESH = pl.DeviceIdType.MESH
BF = jnp.bfloat16
F32 = jnp.float32

PARTS = (
    (0, 176, 96, ("x", "y", "z")),
    (176, 160, 80, ("y", "z", "x")),
    (336, 176, 96, ("z", "x", "y")),
)
Y_UNITS = 5
X_UNITS = 3


def place():
    r = lax.axis_index("replica")
    f = lax.axis_index("fsdp")
    x = (f // 8) * 2 + r // 4
    return x, lax.rem(f // 2, 4), lax.rem(r, 4), lax.rem(f, 2)


def device(x, y, z, c):
    return (lax.rem(x, 2) * 4 + z, (x // 2) * 8 + y * 2 + c)


def up(i, n=4):
    return lax.rem(i + 1, n)


def down(i, n=4):
    return lax.rem(i + n - 1, n)


def remote(src, dst, send, recv, target):
    return pltpu.make_async_remote_copy(
        src_ref=src, dst_ref=dst, send_sem=send, recv_sem=recv, device_id=target, device_id_type=MESH
    )


def greet(targets):
    barrier = pltpu.get_barrier_semaphore()
    for target in targets:
        pl.semaphore_signal(barrier, inc=1, device_id=target, device_id_type=MESH)
    pl.semaphore_wait(barrier, len(targets))


def outer_kernel(
    lp, params, momentum, mask, attn, resid, gain, og,
    par_out, mom_out, w_out, hg_out, at_out,
    lv, pv, mv, dsend, drecv, nsend, nrecv, fsend, frecv, wb, w5, av, rv, ov, hs, hg, atv, stats, st_own, st_other,
    load_sem, mom_sem, d_send, d_recv, n_send, n_recv, f_send, f_recv, w_send, w_recv,
    act_own, act_send, act_recv, g_send, g_recv, s_send, s_recv, out_sem,
):
    x, y, z, c = place()
    r = lax.axis_index("replica")
    f = lax.axis_index("fsdp")
    other = 1 - c
    sibling = device(x, y, z, other)

    xl = lax.rem(x, 2)

    def to_replica(k):
        return (xl + (k // 4) * (1 - 2 * xl)) * 4 + lax.rem(z + k % 4, 4)

    def from_replica(k):
        return (xl + (k // 4) * (1 - 2 * xl)) * 4 + lax.rem(z + 4 - k % 4, 4)

    order = (6, 2, 5, 7, 1, 3, 4, 0)
    for k in order:
        cols = pl.ds(pl.multiple_of(to_replica(k) * 512, 512), 512)
        pltpu.make_async_copy(lp.at[:, cols], lv.at[k], load_sem.at[0, k]).start()
        pltpu.make_async_copy(params.at[:, cols], pv.at[k], load_sem.at[1, k]).start()
    own_cols = pl.ds(pl.multiple_of(r * 512, 512), 512)
    mom_copy = pltpu.make_async_copy(momentum.at[:, own_cols], mv, mom_sem)
    mom_copy.start()

    def plane_peer(j):
        return device(lax.rem(x + j // 4, 4), y, lax.rem(z + j % 4, 4), c)

    def column_peer(j):
        return device(x, lax.rem(y + j // 2, 4), z, c + (j % 2) * (1 - 2 * c))

    greet([plane_peer(j) for j in range(1, 16)] + [column_peer(j) for j in range(1, 8)])

    squares = jnp.zeros((8, 512), F32)
    delta_copies = []

    def send_delta(k):
        copy = remote(dsend.at[k], drecv.at[k], d_send.at[k], d_recv.at[k], (to_replica(k), f))
        copy.start()
        delta_copies.append(copy)

    for k in order:
        pltpu.make_async_copy(lv.at[k], lv.at[k], load_sem.at[0, k]).wait()
        pltpu.make_async_copy(pv.at[k], pv.at[k], load_sem.at[1, k]).wait()
        delta = pv[k] - lv[k]
        squares = squares + jnp.sum((delta * delta).reshape(16, 8, 512), axis=0)
        block = jnp.clip(delta, -BF16_MAX, BF16_MAX).astype(BF)
        if k == 0:
            drecv[0] = block
        else:
            dsend[k] = block
        if k in order[:2]:
            send_delta(k)

    tile = squares[:, 0:128] + squares[:, 128:256] + squares[:, 256:384] + squares[:, 384:512]
    nsend[...] = tile
    nrecv[0] = tile
    norm_copies = []
    for j in range(1, 16):
        copy = remote(nsend, nrecv.at[j], n_send.at[j], n_recv.at[j], plane_peer(j))
        copy.start()
        norm_copies.append(copy)
    for k in order[2:7]:
        send_delta(k)

    mine = pl.ds(pl.multiple_of(c * TOK, TOK), TOK)
    act_copies = []
    attn_own = pltpu.make_async_copy(attn, av.at[mine], act_own.at[0])
    attn_send = remote(attn, av.at[mine], act_send.at[0], act_recv.at[0], sibling)
    attn_own.start()
    attn_send.start()
    for k in range(8):
        for s, (src, dst) in enumerate(((resid, rv), (og, ov))):
            here = pl.ds(pl.multiple_of(k * 512 + c * 256, 256), 256)
            there = pl.ds(pl.multiple_of(k * 512 + other * 256, 256), 256)
            i = 1 + 2 * k + s
            a = pltpu.make_async_copy(src.at[:, here], dst.at[k, mine], act_own.at[i])
            b = remote(src.at[:, there], dst.at[k, mine], act_send.at[i], act_recv.at[i], sibling)
            a.start()
            b.start()
            act_copies.append((a, b))

    for copy in norm_copies:
        copy.wait_recv()
    partial = jnp.concatenate(
        [jnp.sum(nrecv[k] + nrecv[k + 8], axis=0, keepdims=True) for k in range(8)], axis=0
    )
    fsend[...] = partial
    frecv[0] = partial
    factor_copies = []
    for j in range(1, 8):
        copy = remote(fsend, frecv.at[j], f_send.at[j], f_recv.at[j], column_peer(j))
        copy.start()
        factor_copies.append(copy)
    for copy in factor_copies:
        copy.wait_recv()
    limit = clip_scale * math.sqrt(HQ * D)
    norms = jnp.sqrt(jnp.sum(jnp.sum(frecv[...], axis=0), axis=1, keepdims=True))
    factors = jnp.broadcast_to(jnp.minimum(F32(1.0), limit / (norms + 1e-06)), (8, 128))
    count = F32(0.0)
    for k in range(8):
        count = count + mask[k].astype(F32)

    mom_copy.wait()
    pseudo = jnp.zeros((128, 512), F32)
    for k in (0,) + order[:7]:
        if k > 0:
            delta_copies[order.index(k)].wait_recv()
        weight = mask[from_replica(k)].astype(F32) * jnp.max(factors[k : k + 1])
        pseudo = pseudo + drecv[k].astype(F32) * weight
    pseudo = pseudo / count
    new_mom = outer_beta * mv[...] + pseudo
    new_par = pv[0] - outer_rate * (pseudo + outer_beta * new_mom)
    mom_out[...] = new_mom
    par_out[...] = new_par
    rounded = new_par.astype(BF)
    for h in range(2):
        for q in range(2):
            wb[h, q] = rounded[:, h * 256 + q * 128 : h * 256 + q * 128 + 128]

    swaps = []
    for q in range(2):
        rows = pl.ds(pl.multiple_of(q * 256 + c * 128, 128), 128)
        swap = remote(wb.at[other, q], w5.at[x, z, y, rows], w_send.at[q], w_recv.at[q], sibling)
        swap.start()
        swaps.append(swap)
        w5[x, z, y, rows, :] = wb[c, q]
    for swap in swaps:
        swap.wait_recv()

    index = {"x": x, "y": y, "z": z}
    OWN, DOWN, UP, FAR = range(4)

    def at_side(axis, side):
        i = index[axis]
        return (i, down(i), up(i), lax.rem(i + 2, 4))[side]

    def region(part, phase, piece, side, half):
        start, size, cut, axes = PARTS[part]
        if half == 0:
            size = cut
        elif half == 1:
            start, size = start + cut, size - cut
        at = dict(index)
        at[axes[phase]] = at_side(axes[phase], side)
        if phase == 1:
            at[axes[0]] = at_side(axes[0], piece)
        if phase == 2:
            at[axes[0]] = at[axes[1]] = slice(None)
            if part > 0:
                at["z"] = at_side("z", piece)
        return w5.at[at["x"], at["z"], at["y"], pl.ds(start, size), :]

    def sem_of(part, phase, piece, kind):
        return part * 36 + (0, 4, 20)[phase] + piece * 4 + kind

    gather_copies = []

    def send(part, phase, piece, kind, ref):
        axis = PARTS[part][3][phase]
        to = dict(index)
        to[axis] = at_side(axis, UP if kind % 2 == 0 else DOWN)
        sem = sem_of(part, phase, piece, kind)
        copy = remote(ref, ref, g_send.at[sem], g_recv.at[sem], device(to["x"], to["y"], to["z"], c))
        copy.start()
        gather_copies.append(copy)

    def arrived(part, phase, piece, kind, ref):
        pltpu.make_async_copy(ref, ref, g_recv.at[sem_of(part, phase, piece, kind)]).wait()

    def direct(part, phase, piece):
        ref = region(part, phase, piece, OWN, None)
        send(part, phase, piece, 0, ref)
        send(part, phase, piece, 1, ref)

    def sides(part, phase, piece):
        arrived(part, phase, piece, 0, region(part, phase, piece, DOWN, None))
        send(part, phase, piece, 2, region(part, phase, piece, DOWN, 0))
        arrived(part, phase, piece, 1, region(part, phase, piece, UP, None))
        send(part, phase, piece, 3, region(part, phase, piece, UP, 1))

    def far(part, phase, piece):
        arrived(part, phase, piece, 2, region(part, phase, piece, FAR, 0))
        arrived(part, phase, piece, 3, region(part, phase, piece, FAR, 1))

    def hidden(side):
        plane = at_side("z", side)

        @pl.loop(0, 4)
        def _(t):
            half = t // 2
            k = half * 4 + plane
            tok = pl.ds(pl.multiple_of(lax.rem(t, 2) * 512, 512), 512)

            def block(xi):
                both = w5[xi, plane]
                return jnp.concatenate(
                    [both[:, 0:256].reshape(1024, 128), both[:, 256:512].reshape(1024, 128)], axis=1
                )

            h = jnp.dot(av[tok, 0:1024], block(half), preferred_element_type=F32)
            h = h + jnp.dot(av[tok, 1024:2048], block(half + 2), preferred_element_type=F32)
            h = h + rv[k, tok, :].astype(F32)
            hs[k, tok, :] = h
            sc = ov[k, tok, :].astype(F32) * gain[2 * k + c]
            hh = h * h
            sh = sc * h
            stats[0, tok, :] += hh[:, 0:128] + hh[:, 128:256]
            stats[1, tok, :] += sh[:, 0:128] + sh[:, 128:256]

    every = range(3)
    for phase in range(2):
        for part in every:
            direct(part, phase, OWN)
    stats[...] = jnp.zeros_like(stats)
    for part in every:
        arrived(part, 0, 0, 0, region(part, 0, 0, DOWN, None))
        send(part, 0, 0, 2, region(part, 0, 0, DOWN, 0))
        direct(part, 1, DOWN)
        arrived(part, 0, 0, 1, region(part, 0, 0, UP, None))
        send(part, 0, 0, 3, region(part, 0, 0, UP, 1))
        direct(part, 1, UP)
    for part in every:
        far(part, 0, 0)
        direct(part, 1, FAR)
    for piece in range(4):
        for part in every:
            sides(part, 1, piece)
    for piece in range(4):
        for part in every:
            far(part, 1, piece)

    def turn(start, stop):
        @pl.loop(start, stop)
        def _(t):
            tok = pl.ds(pl.multiple_of(lax.rem(t, 4) * 256, 256), 256)
            col = pl.ds(pl.multiple_of((t // 4) * 256, 256), 256)
            atv[t // 4, :, tok] = av[tok, col].T

    direct(1, 2, OWN)
    direct(2, 2, OWN)
    direct(0, 2, OWN)
    direct(1, 2, DOWN)
    direct(2, 2, DOWN)

    attn_own.wait()
    attn_send.wait_recv()
    turn(0, 8)
    for a, b in act_copies:
        a.wait()
        b.wait_recv()
    sides(1, 2, OWN)
    sides(2, 2, OWN)
    direct(1, 2, UP)
    direct(2, 2, UP)
    turn(8, 16)
    sides(1, 2, DOWN)
    sides(2, 2, DOWN)
    direct(1, 2, FAR)
    direct(2, 2, FAR)
    far(1, 2, OWN)
    far(2, 2, OWN)
    hidden(OWN)
    sides(1, 2, UP)
    sides(2, 2, UP)
    sides(0, 2, OWN)
    far(1, 2, DOWN)
    far(2, 2, DOWN)
    hidden(DOWN)
    sides(1, 2, FAR)
    sides(2, 2, FAR)
    far(1, 2, UP)
    far(2, 2, UP)
    hidden(UP)
    turn(16, 32)
    at_copy = pltpu.make_async_copy(atv, at_out, out_sem.at[0])
    at_copy.start()
    far(0, 2, OWN)
    far(1, 2, FAR)
    far(2, 2, FAR)
    w_copy = pltpu.make_async_copy(w5, w_out, out_sem.at[1])
    w_copy.start()
    hidden(FAR)

    lane = lax.broadcasted_iota(jnp.int32, (256, 128), 1)

    @pl.loop(0, 4)
    def _(t):
        tok = pl.ds(pl.multiple_of(t * 256, 256), 256)
        a = jnp.sum(stats[0, tok, :], axis=1, keepdims=True)
        b = jnp.sum(stats[1, tok, :], axis=1, keepdims=True)
        st_own[tok, :] = jnp.where(lane < 64, a, b)

    st_copy = remote(st_own, st_other, s_send, s_recv, sibling)
    st_copy.start()
    st_copy.wait_recv()

    @pl.loop(0, 4)
    def _(t):
        tok = pl.ds(pl.multiple_of(t * 256, 256), 256)
        both = (st_own[tok, :] + st_other[tok, :]) * (1.0 / D)
        inv = lax.rsqrt(both[:, 0:1] + 1e-05)
        slope = inv * inv * inv * both[:, 64:65]
        for k in range(8):
            sc = ov[k, tok, :].astype(F32) * gain[2 * k + c]
            hg[k, tok, :] = (inv * sc - hs[k, tok, :] * slope).astype(BF)

    hg_copy = pltpu.make_async_copy(hg, hg_out, out_sem.at[2])
    hg_copy.start()

    for copy in delta_copies + norm_copies + factor_copies + gather_copies + swaps + [st_copy, attn_send]:
        copy.wait_send()
    for _, b in act_copies:
        b.wait_send()
    at_copy.wait()
    w_copy.wait()
    hg_copy.wait()


def grad_kernel(
    at, hgr, w,
    wg_out, ag_out, hg_out,
    atv, hgv, w5, part, ry, ryx, rx, rxy, fin, agf, ags, agr,
    load_sem, y_send, y_recv, yx_send, yx_recv, x_send, x_recv, xy_send, xy_recv,
    fin_send, fin_recv, ag_send, ag_recv, hgo_own, hgo_send, hgo_recv,
):
    x, y, z, c = place()
    other = 1 - c
    xh = x // 2
    xo = 1 - xh
    sibling = device(x, y, z, other)
    yr, yl, yo = up(y), down(y), lax.rem(y + 2, 4)
    right, left = device(x, yr, z, c), device(x, yl, z, c)
    across = device(lax.rem(x + 2, 4), y, z, c)

    at_load = pltpu.make_async_copy(at, atv, load_sem.at[0])
    hg_load = pltpu.make_async_copy(hgr, hgv, load_sem.at[1])
    w_load = pltpu.make_async_copy(w, w5, load_sem.at[2])
    at_load.start()
    hg_load.start()
    w_load.start()
    greet([sibling, right, left, across])
    at_load.wait()
    hg_load.wait()

    def comp(k, h, d):
        acc = jnp.dot(atv[h * 4 + d], hgv[k], preferred_element_type=F32)
        part[k, h, d] = acc.astype(BF).reshape(2, 128, 256)

    def y_copy(u, m):
        d, h = ((yo, 0), (yo, 1), (yr, 1), (yl, 0), (yr, 0), (yl, 1))[m]
        target = right if m % 2 == 0 else left
        return remote(part.at[u, :, d, h], ry.at[u, m], y_send.at[u, m], y_recv.at[u, m], target)

    def yx_copy(u):
        return remote(part.at[u, xo, y], ryx.at[u], yx_send.at[u], yx_recv.at[u], across)

    def x_copy(v):
        return remote(part.at[Y_UNITS + v, xo], rx.at[v], x_send.at[v], x_recv.at[v], across)

    def xy_copy(v, m):
        d, h = ((yo, 0), (yo, 1), (yr, 1), (yl, 0), (yr, 0), (yl, 1))[m]
        target = right if m % 2 == 0 else left
        return remote(
            part.at[Y_UNITS + v, xh, d, h], rxy.at[v, m], xy_send.at[v, m], xy_recv.at[v, m], target
        )

    def x_start(v):
        for d in range(4):
            comp(Y_UNITS + v, xo, d)
        x_copy(v).start()

    def y_start(u):
        comp(u, 0, yo)
        comp(u, 1, yo)
        y_copy(u, 0).start()
        y_copy(u, 1).start()

    @pl.loop(0, X_UNITS)
    def _(v):
        x_start(v)
        y_start(v)

    @pl.loop(X_UNITS, Y_UNITS)
    def _(u):
        y_start(u)

    @pl.loop(0, Y_UNITS)
    def _(u):
        comp(u, 0, yr)
        comp(u, 1, yr)
        y_copy(u, 2).start()
        comp(u, 0, yl)
        comp(u, 1, yl)
        y_copy(u, 3).start()

    mine = pl.ds(pl.multiple_of(c * TOK, TOK), TOK)
    theirs = pl.ds(pl.multiple_of(other * TOK, TOK), TOK)

    def hgo_copies(k):
        cols = pl.ds(pl.multiple_of(k * 512 + c * 256, 256), 256)
        return (
            pltpu.make_async_copy(hgv.at[k, mine], hg_out.at[:, cols], hgo_own.at[k]),
            remote(hgv.at[k, theirs], hg_out.at[:, cols], hgo_send.at[k], hgo_recv.at[k], sibling),
        )

    @pl.loop(0, 8)
    def _(k):
        a, b = hgo_copies(k)
        a.start()
        b.start()

    @pl.loop(0, Y_UNITS)
    def _(u):
        comp(u, 0, y)
        comp(u, 1, y)

    @pl.loop(0, X_UNITS)
    def _(v):
        for d in range(4):
            comp(Y_UNITS + v, xh, d)

    def add(dst, src):
        part[dst] = (part[dst].astype(F32) + src.astype(F32)).astype(BF)

    @pl.loop(0, Y_UNITS)
    def _(u):
        y_copy(u, 0).wait_recv()
        for h in range(2):
            add((u, h, yr, 0), ry[u, 0, h])
        y_copy(u, 4).start()
        y_copy(u, 1).wait_recv()
        for h in range(2):
            add((u, h, yl, 1), ry[u, 1, h])
        y_copy(u, 5).start()

    def x_middle(v):
        x_copy(v).wait_recv()
        for d in (yo, yr, yl, y):
            for h in range(2):
                add((Y_UNITS + v, xh, d, h), rx[v, d, h])
            if d is yo:
                xy_copy(v, 0).start()
                xy_copy(v, 1).start()
        xy_copy(v, 2).start()
        xy_copy(v, 3).start()

    def y_finish(u):
        for m in (2, 3, 4, 5):
            y_copy(u, m).wait_recv()
        for h in range(2):
            for s, (m, n) in enumerate(((3, 4), (2, 5))):
                total = part[u, h, y, s].astype(F32) + ry[u, m, h].astype(F32) + ry[u, n, h].astype(F32)
                part[u, h, y, s] = total.astype(BF)
        yx_copy(u).start()

    x_middle(0)

    w_load.wait()

    def agrad(q, tok):
        wide = jnp.concatenate(
            [
                w5[(q // 4) * 2 + k // 4, k % 4, lax.rem(q, 4), h * 256 : h * 256 + 256]
                for k in range(8)
                for h in range(2)
            ],
            axis=1,
        )
        rows = jnp.concatenate([hgv[k, tok, :] for k in range(8)], axis=1)
        return lax.dot_general(rows, wide, (((1,), (1,)), ((), ())), preferred_element_type=F32)

    @pl.loop(0, 8)
    def _(q):
        ags[:, pl.ds(pl.multiple_of(q * 256, 256), 256)] = agrad(q, theirs).astype(BF)

    ag_copy = remote(ags, agr, ag_send, ag_recv, sibling)
    ag_copy.start()

    @pl.loop(0, 8)
    def _(q):
        agf[:, pl.ds(pl.multiple_of(q * 256, 256), 256)] = agrad(q, mine)

    ag_copy.wait_recv()

    @pl.loop(0, 8)
    def _(q):
        col = pl.ds(pl.multiple_of(q * 256, 256), 256)
        ag_out[:, col] = (agf[:, col] + agr[:, col].astype(F32)).astype(BF)

    x_middle(1)
    y_finish(0)
    x_middle(2)

    @pl.loop(1, Y_UNITS)
    def _(u):
        y_finish(u)

    @pl.loop(0, X_UNITS)
    def _(v):
        xy_copy(v, 0).wait_recv()
        add((Y_UNITS + v, xh, yr, 0), rxy[v, 0])
        xy_copy(v, 4).start()
        xy_copy(v, 1).wait_recv()
        add((Y_UNITS + v, xh, yl, 1), rxy[v, 1])
        xy_copy(v, 5).start()

    def fin_copy(k):
        cols = pl.ds(pl.multiple_of(k * 512 + c * 256, 256), 256)
        return remote(fin.at[k, other], wg_out.at[:, cols], fin_send.at[k], fin_recv.at[k], sibling)

    def deliver(k):
        fin_copy(k).start()
        cols = pl.ds(pl.multiple_of(k * 512 + c * 256, 256), 256)
        wg_out[:, cols] = fin[k, c]

    @pl.loop(0, Y_UNITS)
    def _(u):
        yx_copy(u).wait_recv()
        fin[u] = (part[u, xh, y].astype(F32) + ryx[u].astype(F32)).astype(BF)
        deliver(u)

    @pl.loop(0, X_UNITS)
    def _(v):
        for m in (2, 3, 4, 5):
            xy_copy(v, m).wait_recv()
        for s, (m, n) in enumerate(((3, 4), (2, 5))):
            total = part[Y_UNITS + v, xh, y, s].astype(F32) + rxy[v, m].astype(F32) + rxy[v, n].astype(F32)
            fin[Y_UNITS + v, s] = total.astype(BF)
        deliver(Y_UNITS + v)

    @pl.loop(0, 8)
    def _(k):
        copy = fin_copy(k)
        copy.wait_recv()
        copy.wait_send()
        a, b = hgo_copies(k)
        a.wait()
        b.wait_recv()
        b.wait_send()

    @pl.loop(0, Y_UNITS)
    def _(u):
        for m in range(6):
            y_copy(u, m).wait_send()
        yx_copy(u).wait_send()

    @pl.loop(0, X_UNITS)
    def _(v):
        x_copy(v).wait_send()
        for m in range(6):
            xy_copy(v, m).wait_send()

    ag_copy.wait_send()


def shards(local_params, params, momentum, old_mask, attn, resid, gain, out_grad):
    hbm = pl.BlockSpec(memory_space=pl.ANY)
    vmem = pl.BlockSpec(memory_space=pltpu.VMEM)
    smem = pl.BlockSpec(memory_space=pltpu.SMEM)
    dma = pltpu.SemaphoreType.DMA
    gains = gain.astype(F32).reshape(16, 1, 256)
    par, mom, w, hg, at = pl.pallas_call(
        outer_kernel,
        out_shape=(
            jax.ShapeDtypeStruct((128, 512), F32),
            jax.ShapeDtypeStruct((128, 512), F32),
            jax.ShapeDtypeStruct((4, 4, 4, 512, 128), BF),
            jax.ShapeDtypeStruct((8, 1024, 256), BF),
            jax.ShapeDtypeStruct((8, 256, 1024), BF),
        ),
        in_specs=[hbm, hbm, hbm, smem, hbm, hbm, vmem, hbm],
        out_specs=(vmem, vmem, hbm, hbm, hbm),
        scratch_shapes=[
            pltpu.VMEM((8, 128, 512), F32),
            pltpu.VMEM((8, 128, 512), F32),
            pltpu.VMEM((128, 512), F32),
            pltpu.VMEM((8, 128, 512), BF),
            pltpu.VMEM((8, 128, 512), BF),
            pltpu.VMEM((8, 128), F32),
            pltpu.VMEM((16, 8, 128), F32),
            pltpu.VMEM((8, 128), F32),
            pltpu.VMEM((8, 8, 128), F32),
            pltpu.VMEM((2, 2, 128, 128), BF),
            pltpu.VMEM((4, 4, 4, 512, 128), BF),
            pltpu.VMEM((1024, 2048), BF),
            pltpu.VMEM((8, 1024, 256), BF),
            pltpu.VMEM((8, 1024, 256), BF),
            pltpu.VMEM((8, 1024, 256), F32),
            pltpu.VMEM((8, 1024, 256), BF),
            pltpu.VMEM((8, 256, 1024), BF),
            pltpu.VMEM((2, 1024, 128), F32),
            pltpu.VMEM((1024, 128), F32),
            pltpu.VMEM((1024, 128), F32),
            dma((2, 8)), dma, dma((8,)), dma((8,)), dma((16,)), dma((16,)), dma((8,)), dma((8,)), dma((2,)), dma((2,)),
            dma((17,)), dma((17,)), dma((17,)), dma((108,)), dma((108,)), dma, dma, dma((3,)),
        ],
        compiler_params=pltpu.CompilerParams(
            collective_id=0, has_side_effects=True, vmem_limit_bytes=56 << 20
        ),
        cost_estimate=pl.CostEstimate(flops=9 * 10**9, bytes_accessed=40 * 2**20, transcendentals=0),
        name="outer_step",
    )(local_params[0], params, momentum, old_mask, attn[0], resid[0], gains, out_grad[0])
    wg, ag, hgo = pl.pallas_call(
        grad_kernel,
        out_shape=(
            jax.ShapeDtypeStruct((128, D), BF),
            jax.ShapeDtypeStruct((TOK, HQ), BF),
            jax.ShapeDtypeStruct((TOK, D), BF),
        ),
        in_specs=[hbm, hbm, hbm],
        out_specs=(vmem, vmem, hbm),
        scratch_shapes=[
            pltpu.VMEM((8, 256, 1024), BF),
            pltpu.VMEM((8, 1024, 256), BF),
            pltpu.VMEM((4, 4, 4, 512, 128), BF),
            pltpu.VMEM((8, 2, 4, 2, 128, 256), BF),
            pltpu.VMEM((Y_UNITS, 6, 2, 128, 256), BF),
            pltpu.VMEM((Y_UNITS, 2, 128, 256), BF),
            pltpu.VMEM((X_UNITS, 4, 2, 128, 256), BF),
            pltpu.VMEM((X_UNITS, 6, 128, 256), BF),
            pltpu.VMEM((8, 2, 128, 256), BF),
            pltpu.VMEM((TOK, HQ), F32),
            pltpu.VMEM((TOK, HQ), BF),
            pltpu.VMEM((TOK, HQ), BF),
            dma((3,)), dma((Y_UNITS, 6)), dma((Y_UNITS, 6)), dma((Y_UNITS,)), dma((Y_UNITS,)),
            dma((X_UNITS,)), dma((X_UNITS,)), dma((X_UNITS, 6)), dma((X_UNITS, 6)),
            dma((8,)), dma((8,)), dma, dma, dma((8,)), dma((8,)), dma((8,)),
        ],
        compiler_params=pltpu.CompilerParams(
            collective_id=1, has_side_effects=True, vmem_limit_bytes=56 << 20
        ),
        cost_estimate=pl.CostEstimate(flops=18 * 10**9, bytes_accessed=40 * 2**20, transcendentals=0),
        name="inner_grads",
    )(at, hg, w)
    return (par, mom, wg[None], ag[None], hgo[None])


def solution(mesh):
    return jax.shard_map(
        shards,
        mesh=mesh,
        in_specs=(
            P("replica", "fsdp", None),
            P("fsdp", None),
            P("fsdp", None),
            P(),
            P("replica", "fsdp", None),
            P("replica", "fsdp", None),
            P(),
            P("replica", "fsdp", None),
        ),
        out_specs=(
            P("fsdp", "replica"),
            P("fsdp", "replica"),
            P("replica", "fsdp", None),
            P("replica", "fsdp", None),
            P("replica", "fsdp", None),
        ),
        check_vma=False,
    )
```

```python
import functools
import math

import jax
import jax.numpy as jnp
from jax import lax
from jax.experimental import pallas as pl
from jax.experimental.pallas import tpu as pltpu
from jax.sharding import PartitionSpec as P

D = 4096
HQ = 2048
TOK = 512

outer_rate = 0.7
outer_beta = 0.9
clip_scale = 0.1
BF16_MAX = float(jnp.finfo(jnp.bfloat16).max)

MESH = pl.DeviceIdType.MESH
BF = jnp.bfloat16
F32 = jnp.float32

PARTS = (
    (0, 176, 96, ("x", "y", "z")),
    (176, 160, 80, ("y", "z", "x")),
    (336, 176, 96, ("z", "x", "y")),
)
Y_UNITS = 5
X_UNITS = 3


def place():
    r = lax.axis_index("replica")
    f = lax.axis_index("fsdp")
    x = (f // 8) * 2 + r // 4
    return x, lax.rem(f // 2, 4), lax.rem(r, 4), lax.rem(f, 2)


def device(x, y, z, c):
    return (lax.rem(x, 2) * 4 + z, (x // 2) * 8 + y * 2 + c)


def up(i, n=4):
    return lax.rem(i + 1, n)


def down(i, n=4):
    return lax.rem(i + n - 1, n)


def remote(src, dst, send, recv, target):
    return pltpu.make_async_remote_copy(
        src_ref=src, dst_ref=dst, send_sem=send, recv_sem=recv, device_id=target, device_id_type=MESH
    )


def greet(targets):
    barrier = pltpu.get_barrier_semaphore()
    for target in targets:
        pl.semaphore_signal(barrier, inc=1, device_id=target, device_id_type=MESH)
    pl.semaphore_wait(barrier, len(targets))


def kernel(
    lp, params, momentum, mask, attn, resid, gain, og,
    par_out, mom_out, wg_out, ag_out, hg_out,
    lv, pv, mv, dsend, drecv, nsend, nrecv, fsend, frecv, wb, w5, av, rv, ov, hs, atv, stats, st_own, st_other,
    part, ry, ryx, rx, rxy, ags, agr,
    load_sem, mom_sem, d_send, d_recv, n_send, n_recv, f_send, f_recv, w_send, w_recv,
    act_own, act_send, act_recv, g_send, g_recv, s_send, s_recv,
    y_send, y_recv, yx_send, yx_recv, x_send, x_recv, xy_send, xy_recv,
    fin_own, fin_send, fin_recv, ag_send, ag_recv, ag_own, hgo_own, hgo_send, hgo_recv,
):
    x, y, z, c = place()
    r = lax.axis_index("replica")
    f = lax.axis_index("fsdp")
    other = 1 - c
    sibling = device(x, y, z, other)

    xl = lax.rem(x, 2)

    def to_replica(k):
        return (xl + (k // 4) * (1 - 2 * xl)) * 4 + lax.rem(z + k % 4, 4)

    def from_replica(k):
        return (xl + (k // 4) * (1 - 2 * xl)) * 4 + lax.rem(z + 4 - k % 4, 4)

    order = (6, 2, 5, 7, 1, 3, 4, 0)
    for k in order:
        cols = pl.ds(pl.multiple_of(to_replica(k) * 512, 512), 512)
        pltpu.make_async_copy(lp.at[:, cols], lv.at[k], load_sem.at[0, k]).start()
        pltpu.make_async_copy(params.at[:, cols], pv.at[k], load_sem.at[1, k]).start()
    own_cols = pl.ds(pl.multiple_of(r * 512, 512), 512)
    mom_copy = pltpu.make_async_copy(momentum.at[:, own_cols], mv, mom_sem)
    mom_copy.start()

    def plane_peer(j):
        return device(lax.rem(x + j // 4, 4), y, lax.rem(z + j % 4, 4), c)

    def column_peer(j):
        return device(x, lax.rem(y + j // 2, 4), z, c + (j % 2) * (1 - 2 * c))

    greet([plane_peer(j) for j in range(1, 16)] + [column_peer(j) for j in range(1, 8)])

    squares = jnp.zeros((8, 512), F32)
    delta_copies = []

    def send_delta(k):
        copy = remote(dsend.at[k], drecv.at[k], d_send.at[k], d_recv.at[k], (to_replica(k), f))
        copy.start()
        delta_copies.append(copy)

    for k in order:
        pltpu.make_async_copy(lv.at[k], lv.at[k], load_sem.at[0, k]).wait()
        pltpu.make_async_copy(pv.at[k], pv.at[k], load_sem.at[1, k]).wait()
        delta = pv[k] - lv[k]
        squares = squares + jnp.sum((delta * delta).reshape(16, 8, 512), axis=0)
        block = jnp.clip(delta, -BF16_MAX, BF16_MAX).astype(BF)
        if k == 0:
            drecv[0, 0] = block[:, 0:256]
            drecv[0, 1] = block[:, 256:512]
        else:
            dsend[k, 0] = block[:, 0:256]
            dsend[k, 1] = block[:, 256:512]
        if k in order[:2]:
            send_delta(k)

    tile = squares[:, 0:128] + squares[:, 128:256] + squares[:, 256:384] + squares[:, 384:512]
    nsend[...] = tile
    nrecv[0] = tile
    norm_copies = []
    for j in range(1, 16):
        copy = remote(nsend, nrecv.at[j], n_send.at[j], n_recv.at[j], plane_peer(j))
        copy.start()
        norm_copies.append(copy)
    for k in order[2:7]:
        send_delta(k)

    mine = pl.ds(pl.multiple_of(c * TOK, TOK), TOK)
    act_copies = []
    attn_own = pltpu.make_async_copy(attn, av.at[mine], act_own.at[0])
    attn_send = remote(attn, av.at[mine], act_send.at[0], act_recv.at[0], sibling)
    attn_own.start()
    attn_send.start()
    for k in range(8):
        for s, (src, dst) in enumerate(((resid, rv), (og, ov))):
            here = pl.ds(pl.multiple_of(k * 512 + c * 256, 256), 256)
            there = pl.ds(pl.multiple_of(k * 512 + other * 256, 256), 256)
            i = 1 + 2 * k + s
            a = pltpu.make_async_copy(src.at[:, here], dst.at[k, mine], act_own.at[i])
            b = remote(src.at[:, there], dst.at[k, mine], act_send.at[i], act_recv.at[i], sibling)
            a.start()
            b.start()
            act_copies.append((a, b))

    for copy in norm_copies:
        copy.wait_recv()
    partial = jnp.concatenate(
        [jnp.sum(nrecv[k] + nrecv[k + 8], axis=0, keepdims=True) for k in range(8)], axis=0
    )
    fsend[...] = partial
    frecv[0] = partial
    factor_copies = []
    for j in range(1, 8):
        copy = remote(fsend, frecv.at[j], f_send.at[j], f_recv.at[j], column_peer(j))
        copy.start()
        factor_copies.append(copy)
    for copy in factor_copies:
        copy.wait_recv()
    limit = clip_scale * math.sqrt(HQ * D)
    norms = jnp.sqrt(jnp.sum(jnp.sum(frecv[...], axis=0), axis=1, keepdims=True))
    factors = jnp.broadcast_to(jnp.minimum(F32(1.0), limit / (norms + 1e-06)), (8, 128))
    count = F32(0.0)
    for k in range(8):
        count = count + mask[k].astype(F32)

    mom_copy.wait()
    pseudo = jnp.zeros((128, 512), F32)
    for k in (0,) + order[:7]:
        if k > 0:
            delta_copies[order.index(k)].wait_recv()
        weight = mask[from_replica(k)].astype(F32) * jnp.max(factors[k : k + 1])
        pseudo = pseudo + jnp.concatenate([drecv[k, 0], drecv[k, 1]], axis=1).astype(F32) * weight
    pseudo = pseudo / count
    new_mom = outer_beta * mv[...] + pseudo
    new_par = pv[0] - outer_rate * (pseudo + outer_beta * new_mom)
    mom_out[...] = new_mom
    par_out[...] = new_par
    rounded = new_par.astype(BF)
    for h in range(2):
        for q in range(2):
            wb[h, q] = rounded[:, h * 256 + q * 128 : h * 256 + q * 128 + 128]

    swaps = []
    for q in range(2):
        rows = pl.ds(pl.multiple_of(q * 256 + c * 128, 128), 128)
        swap = remote(wb.at[other, q], w5.at[x, z, y, rows], w_send.at[q], w_recv.at[q], sibling)
        swap.start()
        swaps.append(swap)
        w5[x, z, y, rows, :] = wb[c, q]
    for swap in swaps:
        swap.wait_recv()

    index = {"x": x, "y": y, "z": z}
    OWN, DOWN, UP, FAR = range(4)

    def at_side(axis, side):
        i = index[axis]
        return (i, down(i), up(i), lax.rem(i + 2, 4))[side]

    def region(p, phase, piece, side, half):
        start, size, cut, axes = PARTS[p]
        if half == 0:
            size = cut
        elif half == 1:
            start, size = start + cut, size - cut
        at = dict(index)
        at[axes[phase]] = at_side(axes[phase], side)
        if phase == 1:
            at[axes[0]] = at_side(axes[0], piece)
        if phase == 2:
            at[axes[0]] = at[axes[1]] = slice(None)
            if p > 0:
                at["z"] = at_side("z", piece)
        return w5.at[at["x"], at["z"], at["y"], pl.ds(start, size), :]

    def sem_of(p, phase, piece, kind):
        return p * 36 + (0, 4, 20)[phase] + piece * 4 + kind

    gather_copies = []

    def send(p, phase, piece, kind, ref):
        axis = PARTS[p][3][phase]
        to = dict(index)
        to[axis] = at_side(axis, UP if kind % 2 == 0 else DOWN)
        sem = sem_of(p, phase, piece, kind)
        copy = remote(ref, ref, g_send.at[sem], g_recv.at[sem], device(to["x"], to["y"], to["z"], c))
        copy.start()
        gather_copies.append(copy)

    def arrived(p, phase, piece, kind, ref):
        pltpu.make_async_copy(ref, ref, g_recv.at[sem_of(p, phase, piece, kind)]).wait()

    def direct(p, phase, piece):
        ref = region(p, phase, piece, OWN, None)
        send(p, phase, piece, 0, ref)
        send(p, phase, piece, 1, ref)

    def sides(p, phase, piece):
        arrived(p, phase, piece, 0, region(p, phase, piece, DOWN, None))
        send(p, phase, piece, 2, region(p, phase, piece, DOWN, 0))
        arrived(p, phase, piece, 1, region(p, phase, piece, UP, None))
        send(p, phase, piece, 3, region(p, phase, piece, UP, 1))

    def far(p, phase, piece):
        arrived(p, phase, piece, 2, region(p, phase, piece, FAR, 0))
        arrived(p, phase, piece, 3, region(p, phase, piece, FAR, 1))

    def hidden(side):
        plane = at_side("z", side)

        @pl.loop(0, 4)
        def _(t):
            half = t // 2
            k = half * 4 + plane
            tok = pl.ds(pl.multiple_of(lax.rem(t, 2) * 512, 512), 512)

            def block(xi):
                both = w5[xi, plane]
                return jnp.concatenate(
                    [both[:, 0:256].reshape(1024, 128), both[:, 256:512].reshape(1024, 128)], axis=1
                )

            h = jnp.dot(av[tok, 0:1024], block(half), preferred_element_type=F32)
            h = h + jnp.dot(av[tok, 1024:2048], block(half + 2), preferred_element_type=F32)
            h = h + rv[k, tok, :].astype(F32)
            hs[k, tok, :] = h
            sc = ov[k, tok, :].astype(F32) * gain[pl.ds(pl.multiple_of(k * 512 + c * 256, 256), 256)].astype(F32)[None, :]
            hh = h * h
            sh = sc * h
            stats[0, tok, :] += hh[:, 0:128] + hh[:, 128:256]
            stats[1, tok, :] += sh[:, 0:128] + sh[:, 128:256]

    every = range(3)
    for phase in range(2):
        for p in every:
            direct(p, phase, OWN)
    stats[...] = jnp.zeros_like(stats)
    for p in every:
        arrived(p, 0, 0, 0, region(p, 0, 0, DOWN, None))
        send(p, 0, 0, 2, region(p, 0, 0, DOWN, 0))
        direct(p, 1, DOWN)
        arrived(p, 0, 0, 1, region(p, 0, 0, UP, None))
        send(p, 0, 0, 3, region(p, 0, 0, UP, 1))
        direct(p, 1, UP)
    for p in every:
        far(p, 0, 0)
        direct(p, 1, FAR)
    for piece in range(4):
        for p in every:
            sides(p, 1, piece)
    for piece in range(4):
        for p in every:
            far(p, 1, piece)

    def turn(start, stop):
        @pl.loop(start, stop)
        def _(t):
            tok = pl.ds(pl.multiple_of(lax.rem(t, 4) * 256, 256), 256)
            col = pl.ds(pl.multiple_of((t // 4) * 256, 256), 256)
            atv[t // 4, :, tok] = av[tok, col].T

    direct(1, 2, OWN)
    direct(2, 2, OWN)
    direct(0, 2, OWN)
    direct(1, 2, DOWN)
    direct(2, 2, DOWN)

    attn_own.wait()
    attn_send.wait_recv()
    turn(0, 8)
    for a, b in act_copies:
        a.wait()
        b.wait_recv()
    sides(1, 2, OWN)
    sides(2, 2, OWN)
    direct(1, 2, UP)
    direct(2, 2, UP)
    turn(8, 16)
    sides(1, 2, DOWN)
    sides(2, 2, DOWN)
    direct(1, 2, FAR)
    direct(2, 2, FAR)
    far(1, 2, OWN)
    far(2, 2, OWN)
    hidden(OWN)
    sides(1, 2, UP)
    sides(2, 2, UP)
    sides(0, 2, OWN)
    far(1, 2, DOWN)
    far(2, 2, DOWN)
    hidden(DOWN)
    sides(1, 2, FAR)
    sides(2, 2, FAR)
    far(1, 2, UP)
    far(2, 2, UP)
    hidden(UP)
    turn(16, 32)
    far(0, 2, OWN)
    far(1, 2, FAR)
    far(2, 2, FAR)
    hidden(FAR)

    lane = lax.broadcasted_iota(jnp.int32, (256, 128), 1)

    @pl.loop(0, 4)
    def _(t):
        tok = pl.ds(pl.multiple_of(t * 256, 256), 256)
        a = jnp.sum(stats[0, tok, :], axis=1, keepdims=True)
        b = jnp.sum(stats[1, tok, :], axis=1, keepdims=True)
        st_own[tok, :] = jnp.where(lane < 64, a, b)

    st_copy = remote(st_own, st_other, s_send, s_recv, sibling)
    st_copy.start()
    st_copy.wait_recv()

    @pl.loop(0, 4)
    def _(t):
        tok = pl.ds(pl.multiple_of(t * 256, 256), 256)
        both = (st_own[tok, :] + st_other[tok, :]) * (1.0 / D)
        inv = lax.rsqrt(both[:, 0:1] + 1e-05)
        stats[0, tok, :] = jnp.broadcast_to(inv, (256, 128))
        stats[1, tok, :] = jnp.broadcast_to(inv * inv * inv * both[:, 64:65], (256, 128))

    hg = rv

    def hgrad(k):
        @pl.loop(0, 4)
        def _(t):
            tok = pl.ds(pl.multiple_of(t * 256, 256), 256)
            sc = ov[k, tok, :].astype(F32) * gain[pl.ds(pl.multiple_of(k * 512 + c * 256, 256), 256)].astype(F32)[None, :]
            inv = jnp.concatenate([stats[0, tok, :]] * 2, axis=1)
            slope = jnp.concatenate([stats[1, tok, :]] * 2, axis=1)
            hg[k, tok, :] = (inv * sc - hs[k, tok, :] * slope).astype(BF)

    xh = x // 2
    xo = 1 - xh
    yr, yl, yo = up(y), down(y), lax.rem(y + 2, 4)
    right, left = device(x, yr, z, c), device(x, yl, z, c)
    across = device(lax.rem(x + 2, 4), y, z, c)

    def comp(k, h, d):
        acc = jnp.dot(atv[h * 4 + d], hg[k], preferred_element_type=F32)
        part[k, h, d] = acc.astype(BF).reshape(2, 128, 256)

    def y_copy(u, m):
        d, h = ((yo, 0), (yo, 1), (yr, 1), (yl, 0), (yr, 0), (yl, 1))[m]
        target = right if m % 2 == 0 else left
        return remote(part.at[u, :, d, h], ry.at[u, m], y_send.at[u, m], y_recv.at[u, m], target)

    def yx_copy(u):
        return remote(part.at[u, xo, y], ryx.at[u], yx_send.at[u], yx_recv.at[u], across)

    def x_copy(v):
        return remote(part.at[Y_UNITS + v, xo], rx.at[v], x_send.at[v], x_recv.at[v], across)

    def xy_copy(v, m):
        d, h = ((yo, 0), (yo, 1), (yr, 1), (yl, 0), (yr, 0), (yl, 1))[m]
        target = right if m % 2 == 0 else left
        return remote(
            part.at[Y_UNITS + v, xh, d, h], rxy.at[v, m], xy_send.at[v, m], xy_recv.at[v, m], target
        )

    def x_start(v):
        hgrad(Y_UNITS + v)
        for d in range(4):
            comp(Y_UNITS + v, xo, d)
        x_copy(v).start()

    def y_start(u):
        hgrad(u)
        comp(u, 0, yo)
        comp(u, 1, yo)
        y_copy(u, 0).start()
        y_copy(u, 1).start()

    @pl.loop(0, X_UNITS)
    def _(v):
        x_start(v)
        y_start(v)

    @pl.loop(X_UNITS, Y_UNITS)
    def _(u):
        y_start(u)

    @pl.loop(0, Y_UNITS)
    def _(u):
        comp(u, 0, yr)
        comp(u, 1, yr)
        y_copy(u, 2).start()
        comp(u, 0, yl)
        comp(u, 1, yl)
        y_copy(u, 3).start()

    theirs = pl.ds(pl.multiple_of(other * TOK, TOK), TOK)

    def hgo_copies(k):
        cols = pl.ds(pl.multiple_of(k * 512 + c * 256, 256), 256)
        return (
            pltpu.make_async_copy(hg.at[k, mine], hg_out.at[:, cols], hgo_own.at[k]),
            remote(hg.at[k, theirs], hg_out.at[:, cols], hgo_send.at[k], hgo_recv.at[k], sibling),
        )

    @pl.loop(0, 8)
    def _(k):
        a, b = hgo_copies(k)
        a.start()
        b.start()

    @pl.loop(0, Y_UNITS)
    def _(u):
        comp(u, 0, y)
        comp(u, 1, y)

    @pl.loop(0, X_UNITS)
    def _(v):
        for d in range(4):
            comp(Y_UNITS + v, xh, d)

    def add(dst, src):
        part[dst] = (part[dst].astype(F32) + src.astype(F32)).astype(BF)

    @pl.loop(0, Y_UNITS)
    def _(u):
        y_copy(u, 0).wait_recv()
        for h in range(2):
            add((u, h, yr, 0), ry[u, 0, h])
        y_copy(u, 4).start()
        y_copy(u, 1).wait_recv()
        for h in range(2):
            add((u, h, yl, 1), ry[u, 1, h])
        y_copy(u, 5).start()

    def x_middle(v):
        x_copy(v).wait_recv()
        for d in (yo, yr, yl, y):
            for h in range(2):
                add((Y_UNITS + v, xh, d, h), rx[v, d, h])
            if d is yo:
                xy_copy(v, 0).start()
                xy_copy(v, 1).start()
        xy_copy(v, 2).start()
        xy_copy(v, 3).start()

    def y_finish(u):
        for m in (2, 3, 4, 5):
            y_copy(u, m).wait_recv()
        for h in range(2):
            for s, (m, n) in enumerate(((3, 4), (2, 5))):
                total = part[u, h, y, s].astype(F32) + ry[u, m, h].astype(F32) + ry[u, n, h].astype(F32)
                part[u, h, y, s] = total.astype(BF)
        yx_copy(u).start()

    x_middle(0)

    def agrad(q, tok):
        wide = jnp.concatenate(
            [
                w5[(q // 4) * 2 + k // 4, k % 4, lax.rem(q, 4), h * 256 : h * 256 + 256]
                for k in range(8)
                for h in range(2)
            ],
            axis=1,
        )
        rows = jnp.concatenate([hg[k, tok, :] for k in range(8)], axis=1)
        return lax.dot_general(rows, wide, (((1,), (1,)), ((), ())), preferred_element_type=F32)

    @pl.loop(0, 8)
    def _(q):
        ags[:, pl.ds(pl.multiple_of(q * 256, 256), 256)] = agrad(q, theirs).astype(BF)

    ag_copy = remote(ags, agr, ag_send, ag_recv, sibling)
    ag_copy.start()

    ag_copy.wait_recv()

    @pl.loop(0, 8)
    def _(q):
        col = pl.ds(pl.multiple_of(q * 256, 256), 256)
        agr[:, col] = (agrad(q, mine) + agr[:, col].astype(F32)).astype(BF)

    ag_store = pltpu.make_async_copy(agr, ag_out, ag_own)
    ag_store.start()

    x_middle(1)
    y_finish(0)
    x_middle(2)

    @pl.loop(1, Y_UNITS)
    def _(u):
        y_finish(u)

    @pl.loop(0, X_UNITS)
    def _(v):
        xy_copy(v, 0).wait_recv()
        add((Y_UNITS + v, xh, yr, 0), rxy[v, 0])
        xy_copy(v, 4).start()
        xy_copy(v, 1).wait_recv()
        add((Y_UNITS + v, xh, yl, 1), rxy[v, 1])
        xy_copy(v, 5).start()

    fin = dsend
    for copy in delta_copies:
        copy.wait_send()

    def fin_copies(k):
        cols = pl.ds(pl.multiple_of(k * 512 + c * 256, 256), 256)
        return (
            pltpu.make_async_copy(fin.at[k, c], wg_out.at[:, cols], fin_own.at[k]),
            remote(fin.at[k, other], wg_out.at[:, cols], fin_send.at[k], fin_recv.at[k], sibling),
        )

    def deliver(k):
        a, b = fin_copies(k)
        a.start()
        b.start()

    @pl.loop(0, Y_UNITS)
    def _(u):
        yx_copy(u).wait_recv()
        fin[u] = (part[u, xh, y].astype(F32) + ryx[u].astype(F32)).astype(BF)
        deliver(u)

    @pl.loop(0, X_UNITS)
    def _(v):
        for m in (2, 3, 4, 5):
            xy_copy(v, m).wait_recv()
        for s, (m, n) in enumerate(((3, 4), (2, 5))):
            total = part[Y_UNITS + v, xh, y, s].astype(F32) + rxy[v, m].astype(F32) + rxy[v, n].astype(F32)
            fin[Y_UNITS + v, s] = total.astype(BF)
        deliver(Y_UNITS + v)

    @pl.loop(0, 8)
    def _(k):
        for a, b in (fin_copies(k), hgo_copies(k)):
            a.wait()
            b.wait_recv()
            b.wait_send()

    @pl.loop(0, Y_UNITS)
    def _(u):
        for m in range(6):
            y_copy(u, m).wait_send()
        yx_copy(u).wait_send()

    @pl.loop(0, X_UNITS)
    def _(v):
        x_copy(v).wait_send()
        for m in range(6):
            xy_copy(v, m).wait_send()

    ag_copy.wait_send()
    ag_store.wait()
    for copy in norm_copies + factor_copies + gather_copies + swaps + [st_copy, attn_send]:
        copy.wait_send()
    for _, b in act_copies:
        b.wait_send()


BLOCKS = ((0, 1), (1, 1), (2, 1), (3, 2), (4, 4))


def hand_over(*refs):
    ins, outs, held, in_sem, out_sem = refs[:5], refs[5:10], refs[10:15], refs[15], refs[16]
    moves = []
    for i, n in BLOCKS:
        rows = ins[i].shape[0] // n
        for j in range(n):
            at = pl.ds(j * rows, rows)
            k = len(moves)
            moves.append(
                (
                    pltpu.make_async_copy(ins[i].at[at], held[i].at[at], in_sem.at[k]),
                    pltpu.make_async_copy(held[i].at[at], outs[i].at[at], out_sem.at[k]),
                )
            )
    for a, _ in moves:
        a.start()
    for a, b in moves:
        a.wait()
        b.start()
    for _, b in moves:
        b.wait()


def shards(local_params, params, momentum, old_mask, attn, resid, gain, out_grad):
    hbm = pl.BlockSpec(memory_space=pl.ANY)
    vmem = pl.BlockSpec(memory_space=pltpu.VMEM)
    smem = pl.BlockSpec(memory_space=pltpu.SMEM)
    dma = pltpu.SemaphoreType.DMA
    par, mom, wg, ag, hg = pl.pallas_call(
        kernel,
        out_shape=(
            jax.ShapeDtypeStruct((128, 512), F32),
            jax.ShapeDtypeStruct((128, 512), F32),
            jax.ShapeDtypeStruct((128, D), BF),
            jax.ShapeDtypeStruct((TOK, HQ), BF),
            jax.ShapeDtypeStruct((TOK, D), BF),
        ),
        in_specs=[hbm, hbm, hbm, smem, hbm, hbm, vmem, hbm],
        out_specs=(vmem, vmem, hbm, hbm, hbm),
        scratch_shapes=[
            pltpu.VMEM((8, 128, 512), F32),
            pltpu.VMEM((8, 128, 512), F32),
            pltpu.VMEM((128, 512), F32),
            pltpu.VMEM((8, 2, 128, 256), BF),
            pltpu.VMEM((8, 2, 128, 256), BF),
            pltpu.VMEM((8, 128), F32),
            pltpu.VMEM((16, 8, 128), F32),
            pltpu.VMEM((8, 128), F32),
            pltpu.VMEM((8, 8, 128), F32),
            pltpu.VMEM((2, 2, 128, 128), BF),
            pltpu.VMEM((4, 4, 4, 512, 128), BF),
            pltpu.VMEM((1024, 2048), BF),
            pltpu.VMEM((8, 1024, 256), BF),
            pltpu.VMEM((8, 1024, 256), BF),
            pltpu.VMEM((8, 1024, 256), F32),
            pltpu.VMEM((8, 256, 1024), BF),
            pltpu.VMEM((2, 1024, 128), F32),
            pltpu.VMEM((1024, 128), F32),
            pltpu.VMEM((1024, 128), F32),
            pltpu.VMEM((8, 2, 4, 2, 128, 256), BF),
            pltpu.VMEM((Y_UNITS, 6, 2, 128, 256), BF),
            pltpu.VMEM((Y_UNITS, 2, 128, 256), BF),
            pltpu.VMEM((X_UNITS, 4, 2, 128, 256), BF),
            pltpu.VMEM((X_UNITS, 6, 128, 256), BF),
            pltpu.VMEM((TOK, HQ), BF),
            pltpu.VMEM((TOK, HQ), BF),
            dma((2, 8)), dma, dma((8,)), dma((8,)), dma((16,)), dma((16,)), dma((8,)), dma((8,)), dma((2,)), dma((2,)),
            dma((17,)), dma((17,)), dma((17,)), dma((108,)), dma((108,)), dma, dma,
            dma((Y_UNITS, 6)), dma((Y_UNITS, 6)), dma((Y_UNITS,)), dma((Y_UNITS,)),
            dma((X_UNITS,)), dma((X_UNITS,)), dma((X_UNITS, 6)), dma((X_UNITS, 6)),
            dma((8,)), dma((8,)), dma((8,)), dma, dma, dma, dma((8,)), dma((8,)), dma((8,)),
        ],
        compiler_params=pltpu.CompilerParams(
            collective_id=0, has_side_effects=True, vmem_limit_bytes=63 << 20
        ),
        cost_estimate=pl.CostEstimate(flops=26 * 10**9, bytes_accessed=40 * 2**20, transcendentals=0),
        name="outer_inner",
    )(local_params[0], params, momentum, old_mask, attn[0], resid[0], gain, out_grad[0])
    par, mom, wg, ag, hg = pl.pallas_call(
        hand_over,
        out_shape=tuple(jax.ShapeDtypeStruct(v.shape, v.dtype) for v in (par, mom, wg, ag, hg)),
        in_specs=[hbm] * 5,
        out_specs=(hbm,) * 5,
        scratch_shapes=[pltpu.VMEM(v.shape, v.dtype) for v in (par, mom, wg, ag, hg)] + [dma((9,)), dma((9,))],
        compiler_params=pltpu.CompilerParams(vmem_limit_bytes=63 << 20),
        name="hand_over",
    )(par, mom, wg, ag, hg)
    return (par, mom, wg[None], ag[None], hg[None])


def solution(mesh):
    return jax.shard_map(
        shards,
        mesh=mesh,
        in_specs=(
            P("replica", "fsdp", None),
            P("fsdp", None),
            P("fsdp", None),
            P(),
            P("replica", "fsdp", None),
            P("replica", "fsdp", None),
            P(),
            P("replica", "fsdp", None),
        ),
        out_specs=(
            P("fsdp", "replica"),
            P("fsdp", "replica"),
            P("replica", "fsdp", None),
            P("replica", "fsdp", None),
            P("replica", "fsdp", None),
        ),
        check_vma=False,
    )
```

```python
import functools
import math

import jax
import jax.numpy as jnp
from jax import lax
from jax.experimental import pallas as pl
from jax.experimental.pallas import tpu as pltpu
from jax.sharding import PartitionSpec as P

D = 4096
HQ = 2048
TOK = 512

outer_rate = 0.7
outer_beta = 0.9
clip_scale = 0.1
BF16_MAX = float(jnp.finfo(jnp.bfloat16).max)

MESH = pl.DeviceIdType.MESH
BF = jnp.bfloat16
F32 = jnp.float32

PARTS = (
    (0, 176, 96, ("x", "y", "z")),
    (176, 160, 80, ("y", "z", "x")),
    (336, 176, 96, ("z", "x", "y")),
)
SPLIT = 4

def place():
    r = lax.axis_index("replica")
    f = lax.axis_index("fsdp")
    x = (f // 8) * 2 + r // 4
    return x, lax.rem(f // 2, 4), lax.rem(r, 4), lax.rem(f, 2)


def device(x, y, z, c):
    return (lax.rem(x, 2) * 4 + z, (x // 2) * 8 + y * 2 + c)


def up(i, n=4):
    return lax.rem(i + 1, n)


def down(i, n=4):
    return lax.rem(i + n - 1, n)


def remote(src, dst, send, recv, target):
    return pltpu.make_async_remote_copy(
        src_ref=src, dst_ref=dst, send_sem=send, recv_sem=recv, device_id=target, device_id_type=MESH
    )


def greet(targets):
    barrier = pltpu.get_barrier_semaphore()
    for target in targets:
        pl.semaphore_signal(barrier, inc=1, device_id=target, device_id_type=MESH)
    return lambda: pl.semaphore_wait(barrier, len(targets))


def kernel(
    lp, params, momentum, mask, attn, resid, gain, og,
    par_out, mom_out, wg_out, ag_out, hg_out,
    mv, nsend, nrecv, fsend, frecv, wb, w5, av, rv, ov, hs, atv, stats, st_other,
    part, ry, ryx, rx, rxy,
    load_sem, mom_sem, d_send, d_recv, n_send, n_recv, f_send, f_recv, w_send, w_recv,
    act_own, act_send, act_recv, g_send, g_recv, s_send, s_recv,
    y_send, y_recv, yx_send, yx_recv, x_send, x_recv, xy_send, xy_recv,
    fin_send, fin_recv, ag_send, ag_recv, hgo_own, hgo_send, hgo_recv,
):
    x, y, z, c = place()
    r = lax.axis_index("replica")
    f = lax.axis_index("fsdp")
    other = 1 - c
    sibling = device(x, y, z, other)

    xl = lax.rem(x, 2)

    def to_replica(k):
        return (xl + (k // 4) * (1 - 2 * xl)) * 4 + lax.rem(z + k % 4, 4)

    def from_replica(k):
        return (xl + (k // 4) * (1 - 2 * xl)) * 4 + lax.rem(z + 4 - k % 4, 4)

    order = (6, 2, 5, 7, 1, 3, 4, 0)

    def loads(k):
        out = []
        for h in range(2):
            cols = pl.ds(pl.multiple_of(to_replica(k) * 512 + h * 256, 256), 256)
            for i, src in enumerate((lp, params)):
                dst = hs.at[k, pl.ds(i * 256 + h * 128, 128)]
                out.append(pltpu.make_async_copy(src.at[:, cols], dst, load_sem.at[2 * h + i, k]))
        return out

    for k in order:
        for load in loads(k):
            load.start()
    own_cols = pl.ds(pl.multiple_of(r * 512, 512), 512)
    mom_copy = pltpu.make_async_copy(momentum.at[:, own_cols], mv, mom_sem)
    mom_copy.start()

    def plane_peer(j):
        return device(lax.rem(x + j // 4, 4), y, lax.rem(z + j % 4, 4), c)

    def column_peer(j):
        return device(x, lax.rem(y + j // 2, 4), z, c + (j % 2) * (1 - 2 * c))

    all_here = greet([plane_peer(j) for j in range(1, 16)] + [column_peer(j) for j in range(1, 8)])

    squares = jnp.zeros((8, 256), F32)
    delta_copies = []

    def block_to(k):
        return atv.at[k, pl.ds(128, 128), pl.ds(0, 512)]

    def block_from(k):
        return atv.at[k, pl.ds(0, 128), pl.ds(0, 512)]

    def send_delta(k):
        copy = remote(block_to(k), block_from(k), d_send.at[k], d_recv.at[k], (to_replica(k), f))
        copy.start()
        delta_copies.append(copy)

    for k in order:
        for load in loads(k):
            load.wait()
        for h in range(2):
            delta = hs[k, 256 + h * 128 : 384 + h * 128, :] - hs[k, h * 128 : 128 + h * 128, :]
            squares = squares + jnp.sum((delta * delta).reshape(16, 8, 256), axis=0)
            block = jnp.clip(delta, -BF16_MAX, BF16_MAX).astype(BF)
            row = 0 if k == 0 else 128
            atv[k, row : row + 128, h * 256 : h * 256 + 256] = block

    tile = squares[:, 0:128] + squares[:, 128:256]
    all_here()
    nsend[...] = tile
    nrecv[0] = tile
    norm_copies = []
    for j in range(1, 16):
        copy = remote(nsend, nrecv.at[j], n_send.at[j], n_recv.at[j], plane_peer(j))
        copy.start()
        norm_copies.append(copy)
    for k in order[:7]:
        send_delta(k)

    mine = pl.ds(pl.multiple_of(c * TOK, TOK), TOK)
    act_copies = []
    attn_own = pltpu.make_async_copy(attn, av.at[mine], act_own.at[0])
    attn_send = remote(attn, av.at[mine], act_send.at[0], act_recv.at[0], sibling)
    attn_own.start()
    attn_send.start()
    for k in range(8):
        for s, (src, dst) in enumerate(((resid, rv), (og, ov))):
            here = pl.ds(pl.multiple_of(k * 512 + c * 256, 256), 256)
            there = pl.ds(pl.multiple_of(k * 512 + other * 256, 256), 256)
            i = 1 + 2 * k + s
            a = pltpu.make_async_copy(src.at[:, here], dst.at[k, mine], act_own.at[i])
            b = remote(src.at[:, there], dst.at[k, mine], act_send.at[i], act_recv.at[i], sibling)
            a.start()
            b.start()
            act_copies.append((a, b))

    for copy in norm_copies:
        copy.wait_recv()
    partial = jnp.concatenate(
        [jnp.sum(nrecv[k] + nrecv[k + 8], axis=0, keepdims=True) for k in range(8)], axis=0
    )
    fsend[...] = partial
    frecv[0] = partial
    factor_copies = []
    for j in range(1, 8):
        copy = remote(fsend, frecv.at[j], f_send.at[j], f_recv.at[j], column_peer(j))
        copy.start()
        factor_copies.append(copy)
    for copy in factor_copies:
        copy.wait_recv()
    limit = clip_scale * math.sqrt(HQ * D)
    norms = jnp.sqrt(jnp.sum(jnp.sum(frecv[...], axis=0), axis=1, keepdims=True))
    factors = jnp.broadcast_to(jnp.minimum(F32(1.0), limit / (norms + 1e-06)), (8, 128))
    count = F32(0.0)
    for k in range(8):
        count = count + mask[k].astype(F32)

    mom_copy.wait()
    pseudo = jnp.zeros((128, 512), F32)
    for k in (0,) + order[:7]:
        if k > 0:
            delta_copies[order.index(k)].wait_recv()
        weight = mask[from_replica(k)].astype(F32) * jnp.max(factors[k : k + 1])
        pseudo = pseudo + atv[k, 0:128, 0:512].astype(F32) * weight
    pseudo = pseudo / count
    new_mom = outer_beta * mv[...] + pseudo
    old_par = jnp.concatenate([hs[0, 256:384, :], hs[0, 384:512, :]], axis=1)
    new_par = old_par - outer_rate * (pseudo + outer_beta * new_mom)
    mom_out[...] = new_mom
    par_out[...] = new_par
    rounded = new_par.astype(BF)
    for h in range(2):
        for q in range(2):
            wb[h, q] = rounded[:, h * 256 + q * 128 : h * 256 + q * 128 + 128]

    swaps = []
    for q in range(2):
        rows = pl.ds(pl.multiple_of(q * 256 + c * 128, 128), 128)
        swap = remote(wb.at[other, q], w5.at[x, z, y, rows], w_send.at[q], w_recv.at[q], sibling)
        swap.start()
        swaps.append(swap)
        w5[x, z, y, rows, :] = wb[c, q]
    for swap in swaps:
        swap.wait_recv()

    index = {"x": x, "y": y, "z": z}
    OWN, DOWN, UP, FAR = range(4)

    def at_side(axis, side):
        i = index[axis]
        return (i, down(i), up(i), lax.rem(i + 2, 4))[side]

    def region(p, phase, piece, side, half):
        start, size, cut, axes = PARTS[p]
        if half == 0:
            size = cut
        elif half == 1:
            start, size = start + cut, size - cut
        at = dict(index)
        at[axes[phase]] = at_side(axes[phase], side)
        if phase == 1:
            at[axes[0]] = at_side(axes[0], piece)
        if phase == 2:
            by = "z" if p > 0 else "y"
            at[axes[0]] = at[axes[1]] = slice(None)
            at[by] = at_side(by, piece)
        return w5.at[at["x"], at["z"], at["y"], pl.ds(start, size), :]

    def sem_of(p, phase, piece, kind):
        return p * 36 + (0, 4, 20)[phase] + piece * 4 + kind

    gather_copies = []

    def send(p, phase, piece, kind, ref):
        axis = PARTS[p][3][phase]
        to = dict(index)
        to[axis] = at_side(axis, UP if kind % 2 == 0 else DOWN)
        sem = sem_of(p, phase, piece, kind)
        copy = remote(ref, ref, g_send.at[sem], g_recv.at[sem], device(to["x"], to["y"], to["z"], c))
        copy.start()
        gather_copies.append(copy)

    def arrived(p, phase, piece, kind, ref):
        pltpu.make_async_copy(ref, ref, g_recv.at[sem_of(p, phase, piece, kind)]).wait()

    def direct(p, phase, piece):
        ref = region(p, phase, piece, OWN, None)
        send(p, phase, piece, 0, ref)
        send(p, phase, piece, 1, ref)

    def sides(p, phase, piece):
        arrived(p, phase, piece, 0, region(p, phase, piece, DOWN, None))
        send(p, phase, piece, 2, region(p, phase, piece, DOWN, 0))
        arrived(p, phase, piece, 1, region(p, phase, piece, UP, None))
        send(p, phase, piece, 3, region(p, phase, piece, UP, 1))

    def far(p, phase, piece):
        arrived(p, phase, piece, 2, region(p, phase, piece, FAR, 0))
        arrived(p, phase, piece, 3, region(p, phase, piece, FAR, 1))

    def hidden(side, only=None):
        plane = at_side("z", side)

        @pl.loop(0, 4 if only is None else 2)
        def _(t):
            half = t // 2 if only is None else t
            k = half * 4 + plane
            part_of = lax.rem(t, 2) if only is None else only
            tok = pl.ds(pl.multiple_of(part_of * 512, 512), 512)

            def block(xi):
                both = w5[xi, plane]
                return jnp.concatenate(
                    [both[:, 0:256].reshape(1024, 128), both[:, 256:512].reshape(1024, 128)], axis=1
                )

            h = jnp.dot(av[tok, 0:1024], block(half), preferred_element_type=F32)
            h = h + jnp.dot(av[tok, 1024:2048], block(half + 2), preferred_element_type=F32)
            h = h + rv[k, tok, :].astype(F32)
            hs[k, tok, :] = h
            sc = ov[k, tok, :].astype(F32) * gain[pl.ds(pl.multiple_of(k * 512 + c * 256, 256), 256)].astype(F32)[None, :]
            hh = h * h
            sh = sc * h
            stats[0, tok, :] += hh[:, 0:128] + hh[:, 128:256]
            stats[1, tok, :] += sh[:, 0:128] + sh[:, 128:256]

    every = range(3)
    for phase in range(2):
        for p in every:
            direct(p, phase, OWN)
    stats[...] = jnp.zeros_like(stats)
    for p in every:
        arrived(p, 0, 0, 0, region(p, 0, 0, DOWN, None))
        send(p, 0, 0, 2, region(p, 0, 0, DOWN, 0))
        direct(p, 1, DOWN)
        arrived(p, 0, 0, 1, region(p, 0, 0, UP, None))
        send(p, 0, 0, 3, region(p, 0, 0, UP, 1))
        direct(p, 1, UP)
    for p in every:
        far(p, 0, 0)
        direct(p, 1, FAR)
    for piece in range(4):
        for p in every:
            sides(p, 1, piece)
    for piece in (OWN, DOWN, UP):
        direct(0, 2, piece)
    direct(1, 2, OWN)
    direct(1, 2, DOWN)
    far(2, 1, OWN)
    direct(2, 2, OWN)
    far(2, 1, DOWN)
    direct(2, 2, DOWN)
    for piece in range(4):
        far(0, 1, piece)
    direct(0, 2, FAR)
    for piece in range(4):
        far(1, 1, piece)
    far(2, 1, UP)
    far(2, 1, FAR)

    def turn(start, stop):
        @pl.loop(start, stop)
        def _(t):
            tok = pl.ds(pl.multiple_of(lax.rem(t, 4) * 256, 256), 256)
            col = pl.ds(pl.multiple_of((t // 4) * 256, 256), 256)
            atv[t // 4, :, tok] = av[tok, col].T

    attn_own.wait()
    attn_send.wait_recv()
    for copy in delta_copies:
        copy.wait_send()
    turn(0, 8)
    for a, b in act_copies:
        a.wait()
        b.wait_recv()
    sides(1, 2, OWN)
    sides(2, 2, OWN)
    direct(1, 2, UP)
    direct(2, 2, UP)
    turn(8, 16)
    sides(1, 2, DOWN)
    sides(2, 2, DOWN)
    direct(1, 2, FAR)
    direct(2, 2, FAR)
    far(1, 2, OWN)
    far(2, 2, OWN)
    hidden(OWN)
    sides(1, 2, UP)
    sides(2, 2, UP)
    for piece in range(4):
        sides(0, 2, piece)
    far(1, 2, DOWN)
    far(2, 2, DOWN)
    hidden(DOWN)
    sides(1, 2, FAR)
    sides(2, 2, FAR)
    far(1, 2, UP)
    far(2, 2, UP)
    hidden(UP)
    turn(16, 32)
    for piece in range(4):
        far(0, 2, piece)
    far(1, 2, FAR)
    far(2, 2, FAR)
    lane = lax.broadcasted_iota(jnp.int32, (256, 128), 1)

    def st_copy(t):
        tok = pl.ds(pl.multiple_of(t * 256, 256), 256)
        return remote(stats.at[0, tok], st_other.at[tok], s_send.at[t], s_recv.at[t], sibling)

    def st_start(first):
        @pl.loop(first, first + 2)
        def _(t):
            tok = pl.ds(pl.multiple_of(t * 256, 256), 256)
            a = jnp.sum(stats[0, tok, :], axis=1, keepdims=True)
            b = jnp.sum(stats[1, tok, :], axis=1, keepdims=True)
            stats[0, tok, :] = jnp.where(lane < 64, a, b)
            st_copy(t).start()

    hidden(FAR, 0)
    st_start(0)
    hidden(FAR, 1)
    st_start(2)

    @pl.loop(0, 4)
    def _(t):
        tok = pl.ds(pl.multiple_of(t * 256, 256), 256)
        st_copy(t).wait()
        both = (stats[0, tok, :] + st_other[tok, :]) * (1.0 / D)
        inv = lax.rsqrt(both[:, 0:1] + 1e-05)
        stats[0, tok, :] = jnp.broadcast_to(inv, (256, 128))
        stats[1, tok, :] = jnp.broadcast_to(inv * inv * inv * both[:, 64:65], (256, 128))

    hg = rv

    def hgrad(k):
        @pl.loop(0, 4)
        def _(t):
            tok = pl.ds(pl.multiple_of(t * 256, 256), 256)
            sc = ov[k, tok, :].astype(F32) * gain[pl.ds(pl.multiple_of(k * 512 + c * 256, 256), 256)].astype(F32)[None, :]
            inv = jnp.concatenate([stats[0, tok, :]] * 2, axis=1)
            slope = jnp.concatenate([stats[1, tok, :]] * 2, axis=1)
            hg[k, tok, :] = (inv * sc - hs[k, tok, :] * slope).astype(BF)

    xh = x // 2
    xo = 1 - xh
    yr, yl, yo = up(y), down(y), lax.rem(y + 2, 4)
    right, left = device(x, yr, z, c), device(x, yl, z, c)
    across = device(lax.rem(x + 2, 4), y, z, c)

    def comp(k, h, d):
        acc = jnp.dot(atv[h * 4 + d], hg[k], preferred_element_type=F32).astype(BF)
        part[k, h, d, :, 0] = acc[:, 0:128].reshape(2, 128, 128)
        part[k, h, d, :, 1] = acc[:, 128:256].reshape(2, 128, 128)

    def cut(ref, *index, q):
        return ref.at[index] if q is None else ref.at[(*index, q)]

    def halves(q):
        return (0, 1) if q is None else (q,)

    every_row = slice(None)

    def y_message(m):
        d, h = ((yo, 0), (yo, 1), (yr, 1), (yl, 0), (yr, 0), (yl, 1))[m]
        return d, h, right if m % 2 == 0 else left

    def y_copy(k, m, q=None):
        d, h, target = y_message(m)
        return remote(
            cut(part, k, every_row, d, h, q=q), cut(ry, k, m, every_row, q=q),
            y_send.at[k, m], y_recv.at[k, m], target,
        )

    def yx_copy(k, q=None):
        return remote(
            cut(part, k, xo, y, every_row, q=q), cut(ryx, k, every_row, q=q), yx_send.at[k], yx_recv.at[k], across
        )

    def x_copy(k, q=None):
        v = k - SPLIT
        return remote(
            cut(part, k, xo, every_row, every_row, q=q), cut(rx, v, every_row, every_row, q=q),
            x_send.at[v], x_recv.at[v], across,
        )

    def xy_copy(k, m, q=None):
        v = k - SPLIT
        d, h, target = y_message(m)
        return remote(
            cut(part, k, xh, d, h, q=q), cut(rxy, v, m, q=q), xy_send.at[v, m], xy_recv.at[v, m], target
        )

    def y_start(k):
        hgrad(k)
        comp(k, 0, yo)
        comp(k, 1, yo)
        y_copy(k, 0).start()
        y_copy(k, 1).start()

    y_start(0)

    @pl.loop(1, SPLIT)
    def _(i):
        k = SPLIT + i
        hgrad(k)
        for d in range(4):
            comp(k, xo, d)
        x_copy(k).start()
        y_start(i)

    hgrad(SPLIT)
    for d in (yo, yr, yl, y):
        comp(SPLIT, 0, d)
        comp(SPLIT, 1, d)
        if d is yo:
            y_copy(SPLIT, 0, 0).start()
            y_copy(SPLIT, 1, 0).start()
    x_copy(SPLIT, 1).start()

    @pl.loop(0, SPLIT)
    def _(k):
        comp(k, 0, yr)
        comp(k, 1, yr)
        y_copy(k, 2).start()
        comp(k, 0, yl)
        comp(k, 1, yl)
        y_copy(k, 3).start()

    y_copy(SPLIT, 2, 0).start()
    y_copy(SPLIT, 3, 0).start()

    theirs = pl.ds(pl.multiple_of(other * TOK, TOK), TOK)

    def hgo_copies(k):
        cols = pl.ds(pl.multiple_of(k * 512 + c * 256, 256), 256)
        return (
            pltpu.make_async_copy(hg.at[k, mine], hg_out.at[:, cols], hgo_own.at[k]),
            remote(hg.at[k, theirs], hg_out.at[:, cols], hgo_send.at[k], hgo_recv.at[k], sibling),
        )

    @pl.loop(0, 8)
    def _(k):
        a, b = hgo_copies(k)
        a.start()
        b.start()

    @pl.loop(0, SPLIT)
    def _(k):
        comp(k, 0, y)
        comp(k, 1, y)

    @pl.loop(SPLIT + 1, 8)
    def _(k):
        for d in range(4):
            comp(k, xh, d)

    def add(dst, *srcs):
        total = part[dst].astype(F32)
        for src in srcs:
            total = total + src.astype(F32)
        part[dst] = total.astype(BF)

    def y_middle(k, q=None):
        for m, d, s in ((0, yr, 0), (1, yl, 1)):
            y_copy(k, m, q).wait_recv()
            for h in range(2):
                for j in halves(q):
                    add((k, h, d, s, j), ry[k, m, h, j])
            y_copy(k, m + 4, q).start()

    def y_finish(k, q=None):
        for m in (2, 3, 4, 5):
            y_copy(k, m, q).wait_recv()
        for h in range(2):
            for s, (m, n) in enumerate(((3, 4), (2, 5))):
                for j in halves(q):
                    add((k, h, y, s, j), ry[k, m, h, j], ry[k, n, h, j])
        yx_copy(k, q).start()

    def x_middle(k, q=None):
        v = k - SPLIT
        x_copy(k, q).wait_recv()
        for d in (yo, yr, yl, y):
            for s in range(2):
                for j in halves(q):
                    add((k, xh, d, s, j), rx[v, d, s, j])
            if d is yo:
                xy_copy(k, 0, q).start()
                xy_copy(k, 1, q).start()
        xy_copy(k, 2, q).start()
        xy_copy(k, 3, q).start()

    def xy_middle(k, q=None):
        v = k - SPLIT
        for m, d, s in ((0, yr, 0), (1, yl, 1)):
            xy_copy(k, m, q).wait_recv()
            for j in halves(q):
                add((k, xh, d, s, j), rxy[v, m, j])
            xy_copy(k, m + 4, q).start()

    @pl.loop(0, SPLIT)
    def _(k):
        y_middle(k)

    y_middle(SPLIT, 0)
    x_middle(SPLIT + 1)

    def agrad(q, tok):
        wide = jnp.concatenate(
            [
                w5[(q // 4) * 2 + k // 4, k % 4, lax.rem(q, 4), h * 256 : h * 256 + 256]
                for k in range(8)
                for h in range(2)
            ],
            axis=1,
        )
        rows = jnp.concatenate([hg[k, tok, :] for k in range(8)], axis=1)
        return lax.dot_general(rows, wide, (((1,), (1,)), ((), ())), preferred_element_type=F32)

    ags = av.at[0:TOK]

    @pl.loop(0, 8)
    def _(i):
        ags[:, pl.ds(pl.multiple_of(i * 256, 256), 256)] = agrad(i, theirs).astype(BF)

    ag_copy = remote(ags, ag_out, ag_send, ag_recv, sibling)
    ag_copy.start()
    ag_copy.wait_recv()

    @pl.loop(0, 8)
    def _(i):
        col = pl.ds(pl.multiple_of(i * 256, 256), 256)
        ag_out[:, col] = (agrad(i, mine) + ag_out[:, col].astype(F32)).astype(BF)

    x_middle(SPLIT + 2)
    y_finish(0)
    y_finish(1)
    x_middle(SPLIT + 3)
    xy_middle(SPLIT + 1)
    y_finish(2)
    y_finish(3)
    y_finish(SPLIT, 0)
    xy_middle(SPLIT + 2)
    x_middle(SPLIT, 1)
    xy_middle(SPLIT + 3)
    xy_middle(SPLIT, 1)

    def fin(k, s):
        return av.at[pl.ds(pl.multiple_of(TOK + s * 128, 128), 128), pl.ds(pl.multiple_of(k * 256, 256), 256)]

    def block_columns(k):
        return pl.ds(pl.multiple_of(k * 512 + c * 256, 256), 256)

    def fin_copy(k):
        return remote(
            fin(k, other), wg_out.at[:, block_columns(k)], fin_send.at[k], fin_recv.at[k], sibling
        )

    def y_total(k, j):
        return part[k, xh, y, :, j].astype(F32) + ryx[k, :, j].astype(F32)

    def x_total(k, j):
        v = k - SPLIT
        rows = [
            part[k, xh, y, s, j].astype(F32) + rxy[v, m, j].astype(F32) + rxy[v, n, j].astype(F32)
            for s, (m, n) in enumerate(((3, 4), (2, 5)))
        ]
        return jnp.stack(rows)

    def deliver(k, left_half, right_half):
        total = jnp.concatenate([left_half, right_half], axis=2).astype(BF)
        fin(k, 0)[...] = total[0]
        fin(k, 1)[...] = total[1]
        fin_copy(k).start()
        wg_out[:, block_columns(k)] = fin(k, c)[...]

    def x_arrive(k, q=None):
        for m in (2, 3, 4, 5):
            xy_copy(k, m, q).wait_recv()

    @pl.loop(0, SPLIT)
    def _(k):
        yx_copy(k).wait_recv()
        deliver(k, y_total(k, 0), y_total(k, 1))

    @pl.loop(SPLIT + 1, 8)
    def _(k):
        x_arrive(k)
        deliver(k, x_total(k, 0), x_total(k, 1))

    yx_copy(SPLIT, 0).wait_recv()
    x_arrive(SPLIT, 1)
    deliver(SPLIT, y_total(SPLIT, 0), x_total(SPLIT, 1))

    @pl.loop(0, 8)
    def _(k):
        a, b = hgo_copies(k)
        a.wait()
        for copy in (b, fin_copy(k)):
            copy.wait_recv()
            copy.wait_send()

    def y_drain(k, q=None):
        for m in range(6):
            y_copy(k, m, q).wait_send()
        yx_copy(k, q).wait_send()

    def x_drain(k, q=None):
        x_copy(k, q).wait_send()
        for m in range(6):
            xy_copy(k, m, q).wait_send()

    @pl.loop(0, SPLIT)
    def _(k):
        y_drain(k)

    @pl.loop(SPLIT + 1, 8)
    def _(k):
        x_drain(k)

    y_drain(SPLIT, 0)
    x_drain(SPLIT, 1)

    ag_copy.wait_send()
    for copy in norm_copies + factor_copies + gather_copies + swaps + [attn_send]:
        copy.wait_send()
    for _, b in act_copies:
        b.wait_send()


def hand_over(*refs):
    sems = refs[10]
    copies = [pltpu.make_async_copy(refs[i], refs[5 + i], sems.at[i]) for i in range(5)]
    for copy in copies:
        copy.start()
    for copy in copies:
        copy.wait()


def shards(local_params, params, momentum, old_mask, attn, resid, gain, out_grad):
    hbm = pl.BlockSpec(memory_space=pl.ANY)
    vmem = pl.BlockSpec(memory_space=pltpu.VMEM)
    smem = pl.BlockSpec(memory_space=pltpu.SMEM)
    dma = pltpu.SemaphoreType.DMA
    par, mom, wg, ag, hg = pl.pallas_call(
        kernel,
        out_shape=(
            pltpu.VMEM((128, 512), F32),
            pltpu.VMEM((128, 512), F32),
            pltpu.VMEM((128, D), BF),
            pltpu.VMEM((TOK, HQ), BF),
            pltpu.VMEM((TOK, D), BF),
        ),
        in_specs=[hbm, hbm, hbm, smem, hbm, hbm, vmem, hbm],
        out_specs=(vmem,) * 5,
        scratch_shapes=[
            pltpu.VMEM((128, 512), F32),
            pltpu.VMEM((8, 128), F32),
            pltpu.VMEM((16, 8, 128), F32),
            pltpu.VMEM((8, 128), F32),
            pltpu.VMEM((8, 8, 128), F32),
            pltpu.VMEM((2, 2, 128, 128), BF),
            pltpu.VMEM((4, 4, 4, 512, 128), BF),
            pltpu.VMEM((1024, 2048), BF),
            pltpu.VMEM((8, 1024, 256), BF),
            pltpu.VMEM((8, 1024, 256), BF),
            pltpu.VMEM((8, 1024, 256), F32),
            pltpu.VMEM((8, 256, 1024), BF),
            pltpu.VMEM((2, 1024, 128), F32),
            pltpu.VMEM((1024, 128), F32),
            pltpu.VMEM((8, 2, 4, 2, 2, 128, 128), BF),
            pltpu.VMEM((SPLIT + 1, 6, 2, 2, 128, 128), BF),
            pltpu.VMEM((SPLIT + 1, 2, 2, 128, 128), BF),
            pltpu.VMEM((8 - SPLIT, 4, 2, 2, 128, 128), BF),
            pltpu.VMEM((8 - SPLIT, 6, 2, 128, 128), BF),
            dma((4, 8)), dma, dma((8,)), dma((8,)), dma((16,)), dma((16,)), dma((8,)), dma((8,)), dma((2,)), dma((2,)),
            dma((17,)), dma((17,)), dma((17,)), dma((108,)), dma((108,)), dma((4,)), dma((4,)),
            dma((SPLIT + 1, 6)), dma((SPLIT + 1, 6)), dma((SPLIT + 1,)), dma((SPLIT + 1,)),
            dma((8 - SPLIT,)), dma((8 - SPLIT,)), dma((8 - SPLIT, 6)), dma((8 - SPLIT, 6)),
            dma((8,)), dma((8,)), dma, dma, dma((8,)), dma((8,)), dma((8,)),
        ],
        compiler_params=pltpu.CompilerParams(
            collective_id=0, has_side_effects=True, vmem_limit_bytes=54 << 20
        ),
        cost_estimate=pl.CostEstimate(flops=26 * 10**9, bytes_accessed=40 * 2**20, transcendentals=0),
        name="outer_inner",
    )(local_params[0], params, momentum, old_mask, attn[0], resid[0], gain, out_grad[0])
    par, mom, wg, ag, hg = pl.pallas_call(
        hand_over,
        out_shape=tuple(jax.ShapeDtypeStruct(v.shape, v.dtype) for v in (par, mom, wg, ag, hg)),
        in_specs=[vmem] * 5,
        out_specs=(hbm,) * 5,
        scratch_shapes=[dma((5,))],
        compiler_params=pltpu.CompilerParams(vmem_limit_bytes=1 << 20),
        name="hand_over",
    )(*(pltpu.with_memory_space_constraint(v, pltpu.VMEM) for v in (par, mom, wg, ag, hg)))
    return (par, mom, wg[None], ag[None], hg[None])


def solution(mesh):
    return jax.shard_map(
        shards,
        mesh=mesh,
        in_specs=(
            P("replica", "fsdp", None),
            P("fsdp", None),
            P("fsdp", None),
            P(),
            P("replica", "fsdp", None),
            P("replica", "fsdp", None),
            P(),
            P("replica", "fsdp", None),
        ),
        out_specs=(
            P("fsdp", "replica"),
            P("fsdp", "replica"),
            P("replica", "fsdp", None),
            P("replica", "fsdp", None),
            P("replica", "fsdp", None),
        ),
        check_vma=False,
    )
```

```python
import functools
import math

import jax
import jax.numpy as jnp
from jax import lax
from jax.experimental import pallas as pl
from jax.experimental.pallas import tpu as pltpu
from jax.sharding import PartitionSpec as P

D = 4096
HQ = 2048
TOK = 512

outer_rate = 0.7
outer_beta = 0.9
clip_scale = 0.1
BF16_MAX = float(jnp.finfo(jnp.bfloat16).max)

MESH = pl.DeviceIdType.MESH
BF = jnp.bfloat16
F32 = jnp.float32

PARTS = (
    (0, 176, 96, ("x", "y", "z")),
    (176, 160, 80, ("y", "z", "x")),
    (336, 176, 96, ("z", "x", "y")),
)
SPLIT = 4

def place():
    r = lax.axis_index("replica")
    f = lax.axis_index("fsdp")
    x = (f // 8) * 2 + r // 4
    return x, lax.rem(f // 2, 4), lax.rem(r, 4), lax.rem(f, 2)


def device(x, y, z, c):
    return (lax.rem(x, 2) * 4 + z, (x // 2) * 8 + y * 2 + c)


def up(i, n=4):
    return lax.rem(i + 1, n)


def down(i, n=4):
    return lax.rem(i + n - 1, n)


def remote(src, dst, send, recv, target):
    return pltpu.make_async_remote_copy(
        src_ref=src, dst_ref=dst, send_sem=send, recv_sem=recv, device_id=target, device_id_type=MESH
    )


def greet(targets):
    barrier = pltpu.get_barrier_semaphore()
    for target in targets:
        pl.semaphore_signal(barrier, inc=1, device_id=target, device_id_type=MESH)
    return lambda: pl.semaphore_wait(barrier, len(targets))


def kernel(
    lp, params, momentum, mask, attn, resid, gain, og,
    par_out, mom_out, wg_out, ag_out, hg_out,
    mv, pv, nsend, nrecv, fsend, frecv, w5, av, rv, ov, hs, atv, stats, st_other,
    part, ry, ryx, rx, rxy,
    load_sem, old_sem, old_send, old_recv, new_send, new_recv, d_send, d_recv, n_send, n_recv, f_send, f_recv,
    act_own, act_send, act_recv, g_send, g_recv, s_send, s_recv,
    y_send, y_recv, yx_send, yx_recv, x_send, x_recv, xy_send, xy_recv,
    fin_send, fin_recv, ag_send, ag_recv, hgo_own, hgo_send, hgo_recv,
):
    x, y, z, c = place()
    r = lax.axis_index("replica")
    f = lax.axis_index("fsdp")
    other = 1 - c
    sibling = device(x, y, z, other)

    xl = lax.rem(x, 2)

    def to_replica(k):
        return (xl + (k // 4) * (1 - 2 * xl)) * 4 + lax.rem(z + k % 4, 4)

    def from_replica(k):
        return (xl + (k // 4) * (1 - 2 * xl)) * 4 + lax.rem(z + 4 - k % 4, 4)

    order = (6, 2, 5, 7, 1, 3, 4, 0)

    def loads(k):
        out = []
        for h in range(2):
            cols = pl.ds(pl.multiple_of(to_replica(k) * 512 + h * 256, 256), 256)
            for i, src in enumerate((lp, params)):
                dst = hs.at[k, pl.ds(i * 256 + h * 128, 128)]
                out.append(pltpu.make_async_copy(src.at[:, cols], dst, load_sem.at[2 * h + i, k]))
        return out

    for k in order:
        for load in loads(k):
            load.start()

    def half_columns(h):
        return pl.ds(pl.multiple_of(r * 512 + h * 256, 256), 256)

    def old_copies(src, dst, i):
        return (
            pltpu.make_async_copy(src.at[:, half_columns(c)], dst.at[:, pl.ds(0, 256)], old_sem.at[i]),
            remote(
                src.at[:, half_columns(other)], dst.at[:, pl.ds(256, 256)], old_send.at[i], old_recv.at[i], sibling
            ),
        )

    old_pairs = [old_copies(momentum, mv, 0), old_copies(params, pv, 1)]
    for own_old, _ in old_pairs:
        own_old.start()

    def plane_peer(j):
        return device(lax.rem(x + j // 4, 4), y, lax.rem(z + j % 4, 4), c)

    def column_peer(j):
        return device(x, lax.rem(y + j // 2, 4), z, c + (j % 2) * (1 - 2 * c))

    def block_peer(k, dc):
        return (to_replica(k), f + dc * (1 - 2 * c))

    all_here = greet(
        [plane_peer(j) for j in range(1, 16)]
        + [column_peer(j) for j in range(1, 8)]
        + [block_peer(k, 1) for k in range(1, 8)]
    )

    squares = jnp.zeros((8, 256), F32)
    delta_copies = []

    def send_delta(k, dc):
        half = c + dc * (1 - 2 * c)
        src = atv.at[k, pl.ds(128, 128), pl.ds(pl.multiple_of(half * 256, 256), 256)]
        dst = atv.at[k, pl.ds(0, 128), pl.ds(dc * 256, 256)]
        copy = remote(src, dst, d_send.at[2 * k + dc], d_recv.at[2 * k + dc], block_peer(k, dc))
        copy.start()
        delta_copies.append(copy)

    for k in order:
        for load in loads(k):
            load.wait()
        for h in range(2):
            delta = hs[k, 256 + h * 128 : 384 + h * 128, :] - hs[k, h * 128 : 128 + h * 128, :]
            squares = squares + jnp.sum((delta * delta).reshape(16, 8, 256), axis=0)
            block = jnp.clip(delta, -BF16_MAX, BF16_MAX).astype(BF)
            atv[k, 128:256, h * 256 : h * 256 + 256] = block
    atv[0, 0:128, 0:256] = atv[0, 128:256, pl.ds(pl.multiple_of(c * 256, 256), 256)]

    tile = squares[:, 0:128] + squares[:, 128:256]
    all_here()
    nsend[...] = tile
    nrecv[0] = tile
    norm_copies = []
    for j in range(1, 16):
        copy = remote(nsend, nrecv.at[j], n_send.at[j], n_recv.at[j], plane_peer(j))
        copy.start()
        norm_copies.append(copy)
    for k in order[:7]:
        for dc in range(2):
            send_delta(k, dc)
    send_delta(0, 1)
    for _, sent_old in old_pairs:
        sent_old.start()

    mine = pl.ds(pl.multiple_of(c * TOK, TOK), TOK)
    act_copies = []
    attn_own = pltpu.make_async_copy(attn, av.at[mine], act_own.at[0])
    attn_send = remote(attn, av.at[mine], act_send.at[0], act_recv.at[0], sibling)
    attn_own.start()
    attn_send.start()
    for k in range(8):
        for s, (src, dst) in enumerate(((resid, rv), (og, ov))):
            here = pl.ds(pl.multiple_of(k * 512 + c * 256, 256), 256)
            there = pl.ds(pl.multiple_of(k * 512 + other * 256, 256), 256)
            i = 1 + 2 * k + s
            a = pltpu.make_async_copy(src.at[:, here], dst.at[k, mine], act_own.at[i])
            b = remote(src.at[:, there], dst.at[k, mine], act_send.at[i], act_recv.at[i], sibling)
            a.start()
            b.start()
            act_copies.append((a, b))

    for copy in norm_copies:
        copy.wait_recv()
    partial = jnp.concatenate(
        [jnp.sum(nrecv[k] + nrecv[k + 8], axis=0, keepdims=True) for k in range(8)], axis=0
    )
    fsend[...] = partial
    frecv[0] = partial
    factor_copies = []
    for j in range(1, 8):
        copy = remote(fsend, frecv.at[j], f_send.at[j], f_recv.at[j], column_peer(j))
        copy.start()
        factor_copies.append(copy)
    for copy in factor_copies:
        copy.wait_recv()
    limit = clip_scale * math.sqrt(HQ * D)
    norms = jnp.sqrt(jnp.sum(jnp.sum(frecv[...], axis=0), axis=1, keepdims=True))
    factors = jnp.broadcast_to(jnp.minimum(F32(1.0), limit / (norms + 1e-06)), (8, 128))
    count = F32(0.0)
    for k in range(8):
        count = count + mask[k].astype(F32)

    pseudo = jnp.zeros((128, 512), F32)
    for copy in delta_copies:
        copy.wait_recv()
    for k in range(8):
        weight = mask[from_replica(k)].astype(F32) * jnp.max(factors[k : k + 1])
        pseudo = pseudo + atv[k, 0:128, 0:512].astype(F32) * weight
    pseudo = pseudo / count
    for own_old, sent_old in old_pairs:
        own_old.wait()
        sent_old.wait_recv()
    new_mom = outer_beta * mv[...] + pseudo
    new_par = pv[...] - outer_rate * (pseudo + outer_beta * new_mom)
    rounded = new_par.astype(BF)

    for dc in range(2):
        for q in range(2):
            rows = pl.ds(pl.multiple_of(q * 256 + (c + dc * (1 - 2 * c)) * 128, 128), 128)
            w5[x, z, y, rows, :] = rounded[:, dc * 256 + q * 128 : dc * 256 + q * 128 + 128]

    index = {"x": x, "y": y, "z": z}
    OWN, DOWN, UP, FAR = range(4)

    def at_side(axis, side):
        i = index[axis]
        return (i, down(i), up(i), lax.rem(i + 2, 4))[side]

    def region(p, phase, piece, side, half):
        start, size, cut, axes = PARTS[p]
        if half == 0:
            size = cut
        elif half == 1:
            start, size = start + cut, size - cut
        at = dict(index)
        at[axes[phase]] = at_side(axes[phase], side)
        if phase == 1:
            at[axes[0]] = at_side(axes[0], piece)
        if phase == 2:
            by = "z" if p > 0 else "y"
            at[axes[0]] = at[axes[1]] = slice(None)
            at[by] = at_side(by, piece)
        return w5.at[at["x"], at["z"], at["y"], pl.ds(start, size), :]

    def sem_of(p, phase, piece, kind):
        return p * 36 + (0, 4, 20)[phase] + piece * 4 + kind

    gather_copies = []

    def send(p, phase, piece, kind, ref):
        axis = PARTS[p][3][phase]
        to = dict(index)
        to[axis] = at_side(axis, UP if kind % 2 == 0 else DOWN)
        sem = sem_of(p, phase, piece, kind)
        copy = remote(ref, ref, g_send.at[sem], g_recv.at[sem], device(to["x"], to["y"], to["z"], c))
        copy.start()
        gather_copies.append(copy)

    def arrived(p, phase, piece, kind, ref):
        pltpu.make_async_copy(ref, ref, g_recv.at[sem_of(p, phase, piece, kind)]).wait()

    def direct(p, phase, piece):
        ref = region(p, phase, piece, OWN, None)
        send(p, phase, piece, 0, ref)
        send(p, phase, piece, 1, ref)

    def sides(p, phase, piece):
        arrived(p, phase, piece, 0, region(p, phase, piece, DOWN, None))
        send(p, phase, piece, 2, region(p, phase, piece, DOWN, 0))
        arrived(p, phase, piece, 1, region(p, phase, piece, UP, None))
        send(p, phase, piece, 3, region(p, phase, piece, UP, 1))

    def far(p, phase, piece):
        arrived(p, phase, piece, 2, region(p, phase, piece, FAR, 0))
        arrived(p, phase, piece, 3, region(p, phase, piece, FAR, 1))

    def hidden(side, only=None):
        plane = at_side("z", side)

        @pl.loop(0, 4 if only is None else 2)
        def _(t):
            half = t // 2 if only is None else t
            k = half * 4 + plane
            part_of = lax.rem(t, 2) if only is None else only
            tok = pl.ds(pl.multiple_of(part_of * 512, 512), 512)

            def block(xi):
                both = w5[xi, plane]
                return jnp.concatenate(
                    [both[:, 0:256].reshape(1024, 128), both[:, 256:512].reshape(1024, 128)], axis=1
                )

            h = jnp.dot(av[tok, 0:1024], block(half), preferred_element_type=F32)
            h = h + jnp.dot(av[tok, 1024:2048], block(half + 2), preferred_element_type=F32)
            h = h + rv[k, tok, :].astype(F32)
            hs[k, tok, :] = h
            sc = ov[k, tok, :].astype(F32) * gain[pl.ds(pl.multiple_of(k * 512 + c * 256, 256), 256)].astype(F32)[None, :]
            hh = h * h
            sh = sc * h
            stats[0, tok, :] += hh[:, 0:128] + hh[:, 128:256]
            stats[1, tok, :] += sh[:, 0:128] + sh[:, 128:256]

    every = range(3)
    for phase in range(2):
        for p in every:
            direct(p, phase, OWN)
    stats[...] = jnp.zeros_like(stats)

    here = pl.ds(pl.multiple_of(c * 256, 256), 256)
    mom_out[:, here] = new_mom[:, 0:256]
    par_out[:, here] = new_par[:, 0:256]
    mv[:, 256:512] = new_mom[:, 256:512]
    pv[:, 256:512] = new_par[:, 256:512]
    new_copies = []
    for i, (src, dst) in enumerate(((mv, mom_out), (pv, par_out))):
        copy = remote(src.at[:, pl.ds(256, 256)], dst.at[:, here], new_send.at[i], new_recv.at[i], sibling)
        copy.start()
        new_copies.append(copy)
    for p in every:
        arrived(p, 0, 0, 0, region(p, 0, 0, DOWN, None))
        send(p, 0, 0, 2, region(p, 0, 0, DOWN, 0))
        direct(p, 1, DOWN)
        arrived(p, 0, 0, 1, region(p, 0, 0, UP, None))
        send(p, 0, 0, 3, region(p, 0, 0, UP, 1))
        direct(p, 1, UP)
    for p in every:
        far(p, 0, 0)
        direct(p, 1, FAR)
    for piece in range(4):
        for p in every:
            sides(p, 1, piece)
    for piece in (OWN, DOWN, UP):
        direct(0, 2, piece)
    direct(1, 2, OWN)
    direct(1, 2, DOWN)
    far(2, 1, OWN)
    direct(2, 2, OWN)
    far(2, 1, DOWN)
    direct(2, 2, DOWN)
    for piece in range(4):
        far(0, 1, piece)
    direct(0, 2, FAR)
    for piece in range(4):
        far(1, 1, piece)
    far(2, 1, UP)
    far(2, 1, FAR)

    def turn(start, stop):
        @pl.loop(start, stop)
        def _(t):
            tok = pl.ds(pl.multiple_of(lax.rem(t, 4) * 256, 256), 256)
            col = pl.ds(pl.multiple_of((t // 4) * 256, 256), 256)
            atv[t // 4, :, tok] = av[tok, col].T

    attn_own.wait()
    attn_send.wait_recv()
    for copy in delta_copies:
        copy.wait_send()
    turn(0, 8)
    for a, b in act_copies:
        a.wait()
        b.wait_recv()
    sides(1, 2, OWN)
    sides(2, 2, OWN)
    direct(1, 2, UP)
    direct(2, 2, UP)
    turn(8, 16)
    sides(1, 2, DOWN)
    sides(2, 2, DOWN)
    direct(1, 2, FAR)
    direct(2, 2, FAR)
    far(1, 2, OWN)
    far(2, 2, OWN)
    hidden(OWN)
    sides(1, 2, UP)
    sides(2, 2, UP)
    for piece in range(4):
        sides(0, 2, piece)
    far(1, 2, DOWN)
    far(2, 2, DOWN)
    hidden(DOWN)
    sides(1, 2, FAR)
    sides(2, 2, FAR)
    far(1, 2, UP)
    far(2, 2, UP)
    hidden(UP)
    turn(16, 32)
    for piece in range(4):
        far(0, 2, piece)
    far(1, 2, FAR)
    far(2, 2, FAR)
    lane = lax.broadcasted_iota(jnp.int32, (256, 128), 1)

    def st_copy(t):
        tok = pl.ds(pl.multiple_of(t * 256, 256), 256)
        return remote(stats.at[0, tok], st_other.at[tok], s_send.at[t], s_recv.at[t], sibling)

    def st_start(first):
        @pl.loop(first, first + 2)
        def _(t):
            tok = pl.ds(pl.multiple_of(t * 256, 256), 256)
            a = jnp.sum(stats[0, tok, :], axis=1, keepdims=True)
            b = jnp.sum(stats[1, tok, :], axis=1, keepdims=True)
            stats[0, tok, :] = jnp.where(lane < 64, a, b)
            st_copy(t).start()

    hidden(FAR, 0)
    st_start(0)
    hidden(FAR, 1)
    st_start(2)

    @pl.loop(0, 4)
    def _(t):
        tok = pl.ds(pl.multiple_of(t * 256, 256), 256)
        st_copy(t).wait()
        both = (stats[0, tok, :] + st_other[tok, :]) * (1.0 / D)
        inv = lax.rsqrt(both[:, 0:1] + 1e-05)
        stats[0, tok, :] = jnp.broadcast_to(inv, (256, 128))
        stats[1, tok, :] = jnp.broadcast_to(inv * inv * inv * both[:, 64:65], (256, 128))

    hg = rv

    def hgrad(k):
        @pl.loop(0, 4)
        def _(t):
            tok = pl.ds(pl.multiple_of(t * 256, 256), 256)
            sc = ov[k, tok, :].astype(F32) * gain[pl.ds(pl.multiple_of(k * 512 + c * 256, 256), 256)].astype(F32)[None, :]
            inv = jnp.concatenate([stats[0, tok, :]] * 2, axis=1)
            slope = jnp.concatenate([stats[1, tok, :]] * 2, axis=1)
            hg[k, tok, :] = (inv * sc - hs[k, tok, :] * slope).astype(BF)

    xh = x // 2
    xo = 1 - xh
    yr, yl, yo = up(y), down(y), lax.rem(y + 2, 4)
    right, left = device(x, yr, z, c), device(x, yl, z, c)
    across = device(lax.rem(x + 2, 4), y, z, c)

    def comp(k, h, d):
        acc = jnp.dot(atv[h * 4 + d], hg[k], preferred_element_type=F32).astype(BF)
        part[k, h, d, :, 0] = acc[:, 0:128].reshape(2, 128, 128)
        part[k, h, d, :, 1] = acc[:, 128:256].reshape(2, 128, 128)

    def cut(ref, *index, q):
        return ref.at[index] if q is None else ref.at[(*index, q)]

    def halves(q):
        return (0, 1) if q is None else (q,)

    every_row = slice(None)

    def y_message(m):
        d, h = ((yo, 0), (yo, 1), (yr, 1), (yl, 0), (yr, 0), (yl, 1))[m]
        return d, h, right if m % 2 == 0 else left

    def y_copy(k, m, q=None):
        d, h, target = y_message(m)
        return remote(
            cut(part, k, every_row, d, h, q=q), cut(ry, k, m, every_row, q=q),
            y_send.at[k, m], y_recv.at[k, m], target,
        )

    def yx_copy(k, q=None):
        return remote(
            cut(part, k, xo, y, every_row, q=q), cut(ryx, k, every_row, q=q), yx_send.at[k], yx_recv.at[k], across
        )

    def x_copy(k, q=None):
        v = k - SPLIT
        return remote(
            cut(part, k, xo, every_row, every_row, q=q), cut(rx, v, every_row, every_row, q=q),
            x_send.at[v], x_recv.at[v], across,
        )

    def xy_copy(k, m, q=None):
        v = k - SPLIT
        d, h, target = y_message(m)
        return remote(
            cut(part, k, xh, d, h, q=q), cut(rxy, v, m, q=q), xy_send.at[v, m], xy_recv.at[v, m], target
        )

    def y_start(k):
        hgrad(k)
        comp(k, 0, yo)
        comp(k, 1, yo)
        y_copy(k, 0).start()
        y_copy(k, 1).start()

    y_start(0)

    @pl.loop(1, SPLIT)
    def _(i):
        k = SPLIT + i
        hgrad(k)
        for d in range(4):
            comp(k, xo, d)
        x_copy(k).start()
        y_start(i)

    hgrad(SPLIT)
    for d in (yo, yr, yl, y):
        comp(SPLIT, 0, d)
        comp(SPLIT, 1, d)
        if d is yo:
            y_copy(SPLIT, 0, 0).start()
            y_copy(SPLIT, 1, 0).start()
    x_copy(SPLIT, 1).start()

    @pl.loop(0, SPLIT)
    def _(k):
        comp(k, 0, yr)
        comp(k, 1, yr)
        y_copy(k, 2).start()
        comp(k, 0, yl)
        comp(k, 1, yl)
        y_copy(k, 3).start()

    y_copy(SPLIT, 2, 0).start()
    y_copy(SPLIT, 3, 0).start()

    theirs = pl.ds(pl.multiple_of(other * TOK, TOK), TOK)

    def hgo_copies(k):
        cols = pl.ds(pl.multiple_of(k * 512 + c * 256, 256), 256)
        return (
            pltpu.make_async_copy(hg.at[k, mine], hg_out.at[:, cols], hgo_own.at[k]),
            remote(hg.at[k, theirs], hg_out.at[:, cols], hgo_send.at[k], hgo_recv.at[k], sibling),
        )

    @pl.loop(0, 8)
    def _(k):
        a, b = hgo_copies(k)
        a.start()
        b.start()

    @pl.loop(0, SPLIT)
    def _(k):
        comp(k, 0, y)
        comp(k, 1, y)

    @pl.loop(SPLIT + 1, 8)
    def _(k):
        for d in range(4):
            comp(k, xh, d)

    def add(dst, *srcs):
        total = part[dst].astype(F32)
        for src in srcs:
            total = total + src.astype(F32)
        part[dst] = total.astype(BF)

    def y_middle(k, q=None):
        for m, d, s in ((0, yr, 0), (1, yl, 1)):
            y_copy(k, m, q).wait_recv()
            for h in range(2):
                for j in halves(q):
                    add((k, h, d, s, j), ry[k, m, h, j])
            y_copy(k, m + 4, q).start()

    def y_finish(k, q=None):
        for m in (2, 3, 4, 5):
            y_copy(k, m, q).wait_recv()
        for h in range(2):
            for s, (m, n) in enumerate(((3, 4), (2, 5))):
                for j in halves(q):
                    add((k, h, y, s, j), ry[k, m, h, j], ry[k, n, h, j])
        yx_copy(k, q).start()

    def x_middle(k, q=None):
        v = k - SPLIT
        x_copy(k, q).wait_recv()
        for d in (yo, yr, yl, y):
            for s in range(2):
                for j in halves(q):
                    add((k, xh, d, s, j), rx[v, d, s, j])
            if d is yo:
                xy_copy(k, 0, q).start()
                xy_copy(k, 1, q).start()
        xy_copy(k, 2, q).start()
        xy_copy(k, 3, q).start()

    def xy_middle(k, q=None):
        v = k - SPLIT
        for m, d, s in ((0, yr, 0), (1, yl, 1)):
            xy_copy(k, m, q).wait_recv()
            for j in halves(q):
                add((k, xh, d, s, j), rxy[v, m, j])
            xy_copy(k, m + 4, q).start()

    @pl.loop(0, SPLIT)
    def _(k):
        y_middle(k)

    y_middle(SPLIT, 0)
    x_middle(SPLIT + 1)

    def agrad(q, tok):
        wide = jnp.concatenate(
            [
                w5[(q // 4) * 2 + k // 4, k % 4, lax.rem(q, 4), h * 256 : h * 256 + 256]
                for k in range(8)
                for h in range(2)
            ],
            axis=1,
        )
        rows = jnp.concatenate([hg[k, tok, :] for k in range(8)], axis=1)
        return lax.dot_general(rows, wide, (((1,), (1,)), ((), ())), preferred_element_type=F32)

    ags = av.at[0:TOK]

    @pl.loop(0, 8)
    def _(i):
        ags[:, pl.ds(pl.multiple_of(i * 256, 256), 256)] = agrad(i, theirs).astype(BF)

    ag_copy = remote(ags, ag_out, ag_send, ag_recv, sibling)
    ag_copy.start()
    ag_copy.wait_recv()

    @pl.loop(0, 8)
    def _(i):
        col = pl.ds(pl.multiple_of(i * 256, 256), 256)
        ag_out[:, col] = (agrad(i, mine) + ag_out[:, col].astype(F32)).astype(BF)

    x_middle(SPLIT + 2)
    y_finish(0)
    y_finish(1)
    x_middle(SPLIT + 3)
    xy_middle(SPLIT + 1)
    y_finish(2)
    y_finish(3)
    y_finish(SPLIT, 0)
    xy_middle(SPLIT + 2)
    x_middle(SPLIT, 1)
    xy_middle(SPLIT + 3)
    xy_middle(SPLIT, 1)

    def fin(k, s):
        return av.at[pl.ds(pl.multiple_of(TOK + s * 128, 128), 128), pl.ds(pl.multiple_of(k * 256, 256), 256)]

    def block_columns(k):
        return pl.ds(pl.multiple_of(k * 512 + c * 256, 256), 256)

    def fin_copy(k):
        return remote(
            fin(k, other), wg_out.at[:, block_columns(k)], fin_send.at[k], fin_recv.at[k], sibling
        )

    def y_total(k, j):
        return part[k, xh, y, :, j].astype(F32) + ryx[k, :, j].astype(F32)

    def x_total(k, j):
        v = k - SPLIT
        rows = [
            part[k, xh, y, s, j].astype(F32) + rxy[v, m, j].astype(F32) + rxy[v, n, j].astype(F32)
            for s, (m, n) in enumerate(((3, 4), (2, 5)))
        ]
        return jnp.stack(rows)

    def deliver(k, left_half, right_half):
        total = jnp.concatenate([left_half, right_half], axis=2).astype(BF)
        fin(k, 0)[...] = total[0]
        fin(k, 1)[...] = total[1]
        fin_copy(k).start()
        wg_out[:, block_columns(k)] = fin(k, c)[...]

    def x_arrive(k, q=None):
        for m in (2, 3, 4, 5):
            xy_copy(k, m, q).wait_recv()

    @pl.loop(0, SPLIT)
    def _(k):
        yx_copy(k).wait_recv()
        deliver(k, y_total(k, 0), y_total(k, 1))

    @pl.loop(SPLIT + 1, 8)
    def _(k):
        x_arrive(k)
        deliver(k, x_total(k, 0), x_total(k, 1))

    yx_copy(SPLIT, 0).wait_recv()
    x_arrive(SPLIT, 1)
    deliver(SPLIT, y_total(SPLIT, 0), x_total(SPLIT, 1))

    @pl.loop(0, 8)
    def _(k):
        a, b = hgo_copies(k)
        a.wait()
        for copy in (b, fin_copy(k)):
            copy.wait_recv()
            copy.wait_send()

    def y_drain(k, q=None):
        for m in range(6):
            y_copy(k, m, q).wait_send()
        yx_copy(k, q).wait_send()

    def x_drain(k, q=None):
        x_copy(k, q).wait_send()
        for m in range(6):
            xy_copy(k, m, q).wait_send()

    @pl.loop(0, SPLIT)
    def _(k):
        y_drain(k)

    @pl.loop(SPLIT + 1, 8)
    def _(k):
        x_drain(k)

    y_drain(SPLIT, 0)
    x_drain(SPLIT, 1)

    ag_copy.wait_send()
    for copy in norm_copies + factor_copies + gather_copies + [attn_send]:
        copy.wait_send()
    for _, sent_old in old_pairs:
        sent_old.wait_send()
    for copy in new_copies:
        copy.wait()
    for _, b in act_copies:
        b.wait_send()


def hand_over(*refs):
    sems = refs[10]
    copies = [pltpu.make_async_copy(refs[i], refs[5 + i], sems.at[i]) for i in range(5)]
    for copy in copies:
        copy.start()
    for copy in copies:
        copy.wait()


def shards(local_params, params, momentum, old_mask, attn, resid, gain, out_grad):
    hbm = pl.BlockSpec(memory_space=pl.ANY)
    vmem = pl.BlockSpec(memory_space=pltpu.VMEM)
    smem = pl.BlockSpec(memory_space=pltpu.SMEM)
    dma = pltpu.SemaphoreType.DMA
    par, mom, wg, ag, hg = pl.pallas_call(
        kernel,
        out_shape=(
            pltpu.VMEM((128, 512), F32),
            pltpu.VMEM((128, 512), F32),
            pltpu.VMEM((128, D), BF),
            pltpu.VMEM((TOK, HQ), BF),
            pltpu.VMEM((TOK, D), BF),
        ),
        in_specs=[hbm, hbm, hbm, smem, hbm, hbm, vmem, hbm],
        out_specs=(vmem,) * 5,
        scratch_shapes=[
            pltpu.VMEM((128, 512), F32),
            pltpu.VMEM((128, 512), F32),
            pltpu.VMEM((8, 128), F32),
            pltpu.VMEM((16, 8, 128), F32),
            pltpu.VMEM((8, 128), F32),
            pltpu.VMEM((8, 8, 128), F32),
            pltpu.VMEM((4, 4, 4, 512, 128), BF),
            pltpu.VMEM((1024, 2048), BF),
            pltpu.VMEM((8, 1024, 256), BF),
            pltpu.VMEM((8, 1024, 256), BF),
            pltpu.VMEM((8, 1024, 256), F32),
            pltpu.VMEM((8, 256, 1024), BF),
            pltpu.VMEM((2, 1024, 128), F32),
            pltpu.VMEM((1024, 128), F32),
            pltpu.VMEM((8, 2, 4, 2, 2, 128, 128), BF),
            pltpu.VMEM((SPLIT + 1, 6, 2, 2, 128, 128), BF),
            pltpu.VMEM((SPLIT + 1, 2, 2, 128, 128), BF),
            pltpu.VMEM((8 - SPLIT, 4, 2, 2, 128, 128), BF),
            pltpu.VMEM((8 - SPLIT, 6, 2, 128, 128), BF),
            dma((4, 8)), dma((2,)), dma((2,)), dma((2,)), dma((2,)), dma((2,)),
            dma((16,)), dma((16,)), dma((16,)), dma((16,)), dma((8,)), dma((8,)),
            dma((17,)), dma((17,)), dma((17,)), dma((108,)), dma((108,)), dma((4,)), dma((4,)),
            dma((SPLIT + 1, 6)), dma((SPLIT + 1, 6)), dma((SPLIT + 1,)), dma((SPLIT + 1,)),
            dma((8 - SPLIT,)), dma((8 - SPLIT,)), dma((8 - SPLIT, 6)), dma((8 - SPLIT, 6)),
            dma((8,)), dma((8,)), dma, dma, dma((8,)), dma((8,)), dma((8,)),
        ],
        compiler_params=pltpu.CompilerParams(
            collective_id=0, has_side_effects=True, vmem_limit_bytes=54 << 20
        ),
        cost_estimate=pl.CostEstimate(flops=26 * 10**9, bytes_accessed=40 * 2**20, transcendentals=0),
        name="outer_inner",
    )(local_params[0], params, momentum, old_mask, attn[0], resid[0], gain, out_grad[0])
    par, mom, wg, ag, hg = pl.pallas_call(
        hand_over,
        out_shape=tuple(jax.ShapeDtypeStruct(v.shape, v.dtype) for v in (par, mom, wg, ag, hg)),
        in_specs=[vmem] * 5,
        out_specs=(hbm,) * 5,
        scratch_shapes=[dma((5,))],
        compiler_params=pltpu.CompilerParams(vmem_limit_bytes=1 << 20),
        name="hand_over",
    )(*(pltpu.with_memory_space_constraint(v, pltpu.VMEM) for v in (par, mom, wg, ag, hg)))
    return (par, mom, wg[None], ag[None], hg[None])


def solution(mesh):
    return jax.shard_map(
        shards,
        mesh=mesh,
        in_specs=(
            P("replica", "fsdp", None),
            P("fsdp", None),
            P("fsdp", None),
            P(),
            P("replica", "fsdp", None),
            P("replica", "fsdp", None),
            P(),
            P("replica", "fsdp", None),
        ),
        out_specs=(
            P("fsdp", "replica"),
            P("fsdp", "replica"),
            P("replica", "fsdp", None),
            P("replica", "fsdp", None),
            P("replica", "fsdp", None),
        ),
        check_vma=False,
    )
```

```python
import functools
import math

import jax
import jax.numpy as jnp
from jax import lax
from jax.experimental import pallas as pl
from jax.experimental.pallas import tpu as pltpu
from jax.sharding import PartitionSpec as P

D = 4096
HQ = 2048
TOK = 512

outer_rate = 0.7
outer_beta = 0.9
clip_scale = 0.1
BF16_MAX = float(jnp.finfo(jnp.bfloat16).max)

MESH = pl.DeviceIdType.MESH
BF = jnp.bfloat16
F32 = jnp.float32

PARTS = (
    (0, 176, 96, ("x", "y", "z")),
    (176, 160, 80, ("y", "z", "x")),
    (336, 176, 96, ("z", "x", "y")),
)
SPLIT = 4

def place():
    r = lax.axis_index("replica")
    f = lax.axis_index("fsdp")
    x = (f // 8) * 2 + r // 4
    return x, lax.rem(f // 2, 4), lax.rem(r, 4), lax.rem(f, 2)


def device(x, y, z, c):
    return (lax.rem(x, 2) * 4 + z, (x // 2) * 8 + y * 2 + c)


def up(i, n=4):
    return lax.rem(i + 1, n)


def down(i, n=4):
    return lax.rem(i + n - 1, n)


def remote(src, dst, send, recv, target):
    return pltpu.make_async_remote_copy(
        src_ref=src, dst_ref=dst, send_sem=send, recv_sem=recv, device_id=target, device_id_type=MESH
    )


def greet(targets):
    barrier = pltpu.get_barrier_semaphore()
    for target in targets:
        pl.semaphore_signal(barrier, inc=1, device_id=target, device_id_type=MESH)
    return lambda: pl.semaphore_wait(barrier, len(targets))


def kernel(
    lp, params, momentum, mask, attn, resid, gain, og,
    par_out, mom_out, wg_out, ag_out, hg_out,
    mv, pv, nsend, nrecv, fsend, frecv, w5, av, rv, ov, hs, atv, stats, st_other,
    part, ry, ryx, rx, rxy,
    load_sem, old_sem, old_send, old_recv, new_send, new_recv, d_send, d_recv, n_send, n_recv, f_send, f_recv,
    act_own, act_send, act_recv, g_send, g_recv, s_send, s_recv,
    y_send, y_recv, yx_send, yx_recv, x_send, x_recv, xy_send, xy_recv,
    fin_send, fin_recv, ag_send, ag_recv, hgo_own, hgo_send, hgo_recv,
):
    x, y, z, c = place()
    r = lax.axis_index("replica")
    f = lax.axis_index("fsdp")
    other = 1 - c
    sibling = device(x, y, z, other)

    xl = lax.rem(x, 2)

    def to_replica(k):
        return (xl + (k // 4) * (1 - 2 * xl)) * 4 + lax.rem(z + k % 4, 4)

    def from_replica(k):
        return (xl + (k // 4) * (1 - 2 * xl)) * 4 + lax.rem(z + 4 - k % 4, 4)

    order = (6, 2, 5, 7, 1, 3, 4, 0)

    def loads(k):
        out = []
        for h in range(2):
            cols = pl.ds(pl.multiple_of(to_replica(k) * 512 + h * 256, 256), 256)
            for i, src in enumerate((lp, params)):
                dst = hs.at[k, pl.ds(i * 256 + h * 128, 128)]
                out.append(pltpu.make_async_copy(src.at[:, cols], dst, load_sem.at[2 * h + i, k]))
        return out

    for k in order:
        for load in loads(k):
            load.start()

    def half_columns(h):
        return pl.ds(pl.multiple_of(r * 512 + h * 256, 256), 256)

    def old_copies(src, dst, i):
        return (
            pltpu.make_async_copy(src.at[:, half_columns(c)], dst.at[:, pl.ds(0, 256)], old_sem.at[i]),
            remote(
                src.at[:, half_columns(other)], dst.at[:, pl.ds(256, 256)], old_send.at[i], old_recv.at[i], sibling
            ),
        )

    old_pairs = [old_copies(momentum, mv, 0), old_copies(params, pv, 1)]
    for own_old, _ in old_pairs:
        own_old.start()

    def plane_peer(j):
        return device(lax.rem(x + j // 4, 4), y, lax.rem(z + j % 4, 4), c)

    def column_peer(j):
        return device(x, lax.rem(y + j // 2, 4), z, c + (j % 2) * (1 - 2 * c))

    def block_peer(k, dc):
        return (to_replica(k), f + dc * (1 - 2 * c))

    all_here = greet(
        [plane_peer(j) for j in range(1, 16)]
        + [column_peer(j) for j in range(1, 8)]
        + [block_peer(k, 1) for k in range(1, 8)]
    )

    squares = jnp.zeros((8, 256), F32)
    delta_copies = []

    def send_delta(k, dc):
        half = c + dc * (1 - 2 * c)
        src = atv.at[k, pl.ds(128, 128), pl.ds(pl.multiple_of(half * 256, 256), 256)]
        dst = atv.at[k, pl.ds(0, 128), pl.ds(dc * 256, 256)]
        copy = remote(src, dst, d_send.at[2 * k + dc], d_recv.at[2 * k + dc], block_peer(k, dc))
        copy.start()
        delta_copies.append(copy)

    for k in order:
        for load in loads(k):
            load.wait()
        for h in range(2):
            delta = hs[k, 256 + h * 128 : 384 + h * 128, :] - hs[k, h * 128 : 128 + h * 128, :]
            squares = squares + jnp.sum((delta * delta).reshape(16, 8, 256), axis=0)
            block = jnp.clip(delta, -BF16_MAX, BF16_MAX).astype(BF)
            atv[k, 128:256, h * 256 : h * 256 + 256] = block
    atv[0, 0:128, 0:256] = atv[0, 128:256, pl.ds(pl.multiple_of(c * 256, 256), 256)]

    tile = squares[:, 0:128] + squares[:, 128:256]
    all_here()
    nsend[...] = tile
    nrecv[0] = tile
    norm_copies = []
    for j in range(1, 16):
        copy = remote(nsend, nrecv.at[j], n_send.at[j], n_recv.at[j], plane_peer(j))
        copy.start()
        norm_copies.append(copy)
    for k in order[:7]:
        for dc in range(2):
            send_delta(k, dc)
    send_delta(0, 1)
    for _, sent_old in old_pairs:
        sent_old.start()

    mine = pl.ds(pl.multiple_of(c * TOK, TOK), TOK)
    act_copies = []
    attn_own = pltpu.make_async_copy(attn, av.at[mine], act_own.at[0])
    attn_send = remote(attn, av.at[mine], act_send.at[0], act_recv.at[0], sibling)
    attn_own.start()
    attn_send.start()
    for k in range(8):
        for s, (src, dst) in enumerate(((resid, rv), (og, ov))):
            here = pl.ds(pl.multiple_of(k * 512 + c * 256, 256), 256)
            there = pl.ds(pl.multiple_of(k * 512 + other * 256, 256), 256)
            i = 1 + 2 * k + s
            a = pltpu.make_async_copy(src.at[:, here], dst.at[k, mine], act_own.at[i])
            b = remote(src.at[:, there], dst.at[k, mine], act_send.at[i], act_recv.at[i], sibling)
            a.start()
            b.start()
            act_copies.append((a, b))

    for copy in norm_copies:
        copy.wait_recv()
    partial = jnp.concatenate(
        [jnp.sum(nrecv[k] + nrecv[k + 8], axis=0, keepdims=True) for k in range(8)], axis=0
    )
    fsend[...] = partial
    frecv[0] = partial
    factor_copies = []
    for j in range(1, 8):
        copy = remote(fsend, frecv.at[j], f_send.at[j], f_recv.at[j], column_peer(j))
        copy.start()
        factor_copies.append(copy)
    for copy in factor_copies:
        copy.wait_recv()
    limit = clip_scale * math.sqrt(HQ * D)
    norms = jnp.sqrt(jnp.sum(jnp.sum(frecv[...], axis=0), axis=1, keepdims=True))
    factors = jnp.broadcast_to(jnp.minimum(F32(1.0), limit / (norms + 1e-06)), (8, 128))
    count = F32(0.0)
    for k in range(8):
        count = count + mask[k].astype(F32)

    pseudo = jnp.zeros((128, 512), F32)
    for copy in delta_copies:
        copy.wait_recv()
    for k in range(8):
        weight = mask[from_replica(k)].astype(F32) * jnp.max(factors[k : k + 1])
        pseudo = pseudo + atv[k, 0:128, 0:512].astype(F32) * weight
    pseudo = pseudo / count
    for own_old, sent_old in old_pairs:
        own_old.wait()
        sent_old.wait_recv()
    new_mom = outer_beta * mv[...] + pseudo
    new_par = pv[...] - outer_rate * (pseudo + outer_beta * new_mom)
    rounded = new_par.astype(BF)

    for dc in range(2):
        for q in range(2):
            rows = pl.ds(pl.multiple_of(q * 256 + (c + dc * (1 - 2 * c)) * 128, 128), 128)
            w5[x, z, y, rows, :] = rounded[:, dc * 256 + q * 128 : dc * 256 + q * 128 + 128]

    index = {"x": x, "y": y, "z": z}
    OWN, DOWN, UP, FAR = range(4)

    def at_side(axis, side):
        i = index[axis]
        return (i, down(i), up(i), lax.rem(i + 2, 4))[side]

    def region(p, phase, piece, side, half):
        start, size, cut, axes = PARTS[p]
        if half == 0:
            size = cut
        elif half == 1:
            start, size = start + cut, size - cut
        at = dict(index)
        at[axes[phase]] = at_side(axes[phase], side)
        if phase == 1:
            at[axes[0]] = at_side(axes[0], piece)
        if phase == 2:
            by = "z" if p > 0 else "y"
            at[axes[0]] = at[axes[1]] = slice(None)
            at[by] = at_side(by, piece)
        return w5.at[at["x"], at["z"], at["y"], pl.ds(start, size), :]

    def sem_of(p, phase, piece, kind):
        return p * 36 + (0, 4, 20)[phase] + piece * 4 + kind

    gather_copies = []

    def send(p, phase, piece, kind, ref):
        axis = PARTS[p][3][phase]
        to = dict(index)
        to[axis] = at_side(axis, UP if kind % 2 == 0 else DOWN)
        sem = sem_of(p, phase, piece, kind)
        copy = remote(ref, ref, g_send.at[sem], g_recv.at[sem], device(to["x"], to["y"], to["z"], c))
        copy.start()
        gather_copies.append(copy)

    def arrived(p, phase, piece, kind, ref):
        pltpu.make_async_copy(ref, ref, g_recv.at[sem_of(p, phase, piece, kind)]).wait()

    def direct(p, phase, piece):
        ref = region(p, phase, piece, OWN, None)
        send(p, phase, piece, 0, ref)
        send(p, phase, piece, 1, ref)

    def sides(p, phase, piece):
        arrived(p, phase, piece, 0, region(p, phase, piece, DOWN, None))
        send(p, phase, piece, 2, region(p, phase, piece, DOWN, 0))
        arrived(p, phase, piece, 1, region(p, phase, piece, UP, None))
        send(p, phase, piece, 3, region(p, phase, piece, UP, 1))

    def far(p, phase, piece):
        arrived(p, phase, piece, 2, region(p, phase, piece, FAR, 0))
        arrived(p, phase, piece, 3, region(p, phase, piece, FAR, 1))

    def hidden(side, only=None):
        plane = at_side("z", side)

        @pl.loop(0, 4 if only is None else 2)
        def _(t):
            half = t // 2 if only is None else t
            k = half * 4 + plane
            part_of = lax.rem(t, 2) if only is None else only
            tok = pl.ds(pl.multiple_of(part_of * 512, 512), 512)

            def block(xi):
                both = w5[xi, plane]
                return jnp.concatenate(
                    [both[:, 0:256].reshape(1024, 128), both[:, 256:512].reshape(1024, 128)], axis=1
                )

            h = jnp.dot(av[tok, 0:1024], block(half), preferred_element_type=F32)
            h = h + jnp.dot(av[tok, 1024:2048], block(half + 2), preferred_element_type=F32)
            h = h + rv[k, tok, :].astype(F32)
            hs[k, tok, :] = h
            sc = ov[k, tok, :].astype(F32) * gain[pl.ds(pl.multiple_of(k * 512 + c * 256, 256), 256)].astype(F32)[None, :]
            hh = h * h
            sh = sc * h
            stats[0, tok, :] += hh[:, 0:128] + hh[:, 128:256]
            stats[1, tok, :] += sh[:, 0:128] + sh[:, 128:256]

    every = range(3)
    for phase in range(2):
        for p in every:
            direct(p, phase, OWN)
    stats[...] = jnp.zeros_like(stats)

    here = pl.ds(pl.multiple_of(c * 256, 256), 256)
    mom_out[:, here] = new_mom[:, 0:256]
    par_out[:, here] = new_par[:, 0:256]
    mv[:, 256:512] = new_mom[:, 256:512]
    pv[:, 256:512] = new_par[:, 256:512]
    new_copies = []
    for i, (src, dst) in enumerate(((mv, mom_out), (pv, par_out))):
        copy = remote(src.at[:, pl.ds(256, 256)], dst.at[:, here], new_send.at[i], new_recv.at[i], sibling)
        copy.start()
        new_copies.append(copy)
    for p in every:
        arrived(p, 0, 0, 0, region(p, 0, 0, DOWN, None))
        send(p, 0, 0, 2, region(p, 0, 0, DOWN, 0))
        direct(p, 1, DOWN)
        arrived(p, 0, 0, 1, region(p, 0, 0, UP, None))
        send(p, 0, 0, 3, region(p, 0, 0, UP, 1))
        direct(p, 1, UP)
    for p in every:
        far(p, 0, 0)
        direct(p, 1, FAR)
    for piece in range(4):
        for p in every:
            sides(p, 1, piece)
    for piece in (OWN, DOWN, UP):
        direct(0, 2, piece)
    direct(1, 2, OWN)
    direct(1, 2, DOWN)
    far(2, 1, OWN)
    direct(2, 2, OWN)
    far(2, 1, DOWN)
    direct(2, 2, DOWN)
    for piece in range(4):
        far(0, 1, piece)
    direct(0, 2, FAR)
    for piece in range(4):
        far(1, 1, piece)
    far(2, 1, UP)
    far(2, 1, FAR)

    def turn(start, stop):
        @pl.loop(start, stop)
        def _(t):
            tok = pl.ds(pl.multiple_of(lax.rem(t, 4) * 256, 256), 256)
            col = pl.ds(pl.multiple_of((t // 4) * 256, 256), 256)
            atv[t // 4, :, tok] = av[tok, col].T

    attn_own.wait()
    attn_send.wait_recv()
    for copy in delta_copies:
        copy.wait_send()
    turn(0, 8)
    for a, b in act_copies:
        a.wait()
        b.wait_recv()
    sides(1, 2, OWN)
    sides(2, 2, OWN)
    direct(1, 2, UP)
    direct(2, 2, UP)
    turn(8, 16)
    sides(1, 2, DOWN)
    sides(2, 2, DOWN)
    direct(1, 2, FAR)
    direct(2, 2, FAR)
    far(1, 2, OWN)
    far(2, 2, OWN)
    hidden(OWN)
    turn(16, 24)
    sides(1, 2, UP)
    sides(2, 2, UP)
    for piece in range(4):
        sides(0, 2, piece)
    far(1, 2, DOWN)
    far(2, 2, DOWN)
    hidden(DOWN)
    turn(24, 32)
    sides(1, 2, FAR)
    sides(2, 2, FAR)
    far(1, 2, UP)
    far(2, 2, UP)
    hidden(UP)
    for piece in range(4):
        far(0, 2, piece)
    far(1, 2, FAR)
    far(2, 2, FAR)
    lane = lax.broadcasted_iota(jnp.int32, (256, 128), 1)

    def st_copy(t):
        tok = pl.ds(pl.multiple_of(t * 256, 256), 256)
        return remote(stats.at[0, tok], st_other.at[tok], s_send.at[t], s_recv.at[t], sibling)

    def st_start(first):
        @pl.loop(first, first + 2)
        def _(t):
            tok = pl.ds(pl.multiple_of(t * 256, 256), 256)
            a = jnp.sum(stats[0, tok, :], axis=1, keepdims=True)
            b = jnp.sum(stats[1, tok, :], axis=1, keepdims=True)
            stats[0, tok, :] = jnp.where(lane < 64, a, b)
            st_copy(t).start()

    hidden(FAR, 0)
    st_start(0)
    hidden(FAR, 1)
    st_start(2)

    @pl.loop(0, 4)
    def _(t):
        tok = pl.ds(pl.multiple_of(t * 256, 256), 256)
        st_copy(t).wait()
        both = (stats[0, tok, :] + st_other[tok, :]) * (1.0 / D)
        inv = lax.rsqrt(both[:, 0:1] + 1e-05)
        stats[0, tok, :] = jnp.broadcast_to(inv, (256, 128))
        stats[1, tok, :] = jnp.broadcast_to(inv * inv * inv * both[:, 64:65], (256, 128))

    hg = rv

    def hgrad(k):
        @pl.loop(0, 4)
        def _(t):
            tok = pl.ds(pl.multiple_of(t * 256, 256), 256)
            sc = ov[k, tok, :].astype(F32) * gain[pl.ds(pl.multiple_of(k * 512 + c * 256, 256), 256)].astype(F32)[None, :]
            inv = jnp.concatenate([stats[0, tok, :]] * 2, axis=1)
            slope = jnp.concatenate([stats[1, tok, :]] * 2, axis=1)
            hg[k, tok, :] = (inv * sc - hs[k, tok, :] * slope).astype(BF)

    xh = x // 2
    xo = 1 - xh
    yr, yl, yo = up(y), down(y), lax.rem(y + 2, 4)
    right, left = device(x, yr, z, c), device(x, yl, z, c)
    across = device(lax.rem(x + 2, 4), y, z, c)

    def comp(k, h, d):
        acc = jnp.dot(atv[h * 4 + d], hg[k], preferred_element_type=F32).astype(BF)
        part[k, h, d, :, 0] = acc[:, 0:128].reshape(2, 128, 128)
        part[k, h, d, :, 1] = acc[:, 128:256].reshape(2, 128, 128)

    def cut(ref, *index, q):
        return ref.at[index] if q is None else ref.at[(*index, q)]

    def halves(q):
        return (0, 1) if q is None else (q,)

    every_row = slice(None)

    def y_message(m):
        d, h = ((yo, 0), (yo, 1), (yr, 1), (yl, 0), (yr, 0), (yl, 1))[m]
        return d, h, right if m % 2 == 0 else left

    def y_copy(k, m, q=None):
        d, h, target = y_message(m)
        return remote(
            cut(part, k, every_row, d, h, q=q), cut(ry, k, m, every_row, q=q),
            y_send.at[k, m], y_recv.at[k, m], target,
        )

    def yx_copy(k, q=None):
        return remote(
            cut(part, k, xo, y, every_row, q=q), cut(ryx, k, every_row, q=q), yx_send.at[k], yx_recv.at[k], across
        )

    def x_copy(k, q=None):
        v = k - SPLIT
        return remote(
            cut(part, k, xo, every_row, every_row, q=q), cut(rx, v, every_row, every_row, q=q),
            x_send.at[v], x_recv.at[v], across,
        )

    def xy_copy(k, m, q=None):
        v = k - SPLIT
        d, h, target = y_message(m)
        return remote(
            cut(part, k, xh, d, h, q=q), cut(rxy, v, m, q=q), xy_send.at[v, m], xy_recv.at[v, m], target
        )

    def y_start(k):
        hgrad(k)
        comp(k, 0, yo)
        comp(k, 1, yo)
        y_copy(k, 0).start()
        y_copy(k, 1).start()

    y_start(0)

    @pl.loop(1, SPLIT)
    def _(i):
        k = SPLIT + i
        hgrad(k)
        for d in range(4):
            comp(k, xo, d)
        x_copy(k).start()
        y_start(i)

    hgrad(SPLIT)
    for d in (yo, yr, yl, y):
        comp(SPLIT, 0, d)
        comp(SPLIT, 1, d)
        if d is yo:
            y_copy(SPLIT, 0, 0).start()
            y_copy(SPLIT, 1, 0).start()
    x_copy(SPLIT, 1).start()

    @pl.loop(0, SPLIT)
    def _(k):
        comp(k, 0, yr)
        comp(k, 1, yr)
        y_copy(k, 2).start()
        comp(k, 0, yl)
        comp(k, 1, yl)
        y_copy(k, 3).start()

    y_copy(SPLIT, 2, 0).start()
    y_copy(SPLIT, 3, 0).start()

    theirs = pl.ds(pl.multiple_of(other * TOK, TOK), TOK)

    def hgo_copies(k):
        cols = pl.ds(pl.multiple_of(k * 512 + c * 256, 256), 256)
        return (
            pltpu.make_async_copy(hg.at[k, mine], hg_out.at[:, cols], hgo_own.at[k]),
            remote(hg.at[k, theirs], hg_out.at[:, cols], hgo_send.at[k], hgo_recv.at[k], sibling),
        )

    @pl.loop(0, 8)
    def _(k):
        a, b = hgo_copies(k)
        a.start()
        b.start()

    @pl.loop(0, SPLIT)
    def _(k):
        comp(k, 0, y)
        comp(k, 1, y)

    @pl.loop(SPLIT + 1, 8)
    def _(k):
        for d in range(4):
            comp(k, xh, d)

    def add(dst, *srcs):
        total = part[dst].astype(F32)
        for src in srcs:
            total = total + src.astype(F32)
        part[dst] = total.astype(BF)

    def y_middle(k, q=None):
        for m, d, s in ((0, yr, 0), (1, yl, 1)):
            y_copy(k, m, q).wait_recv()
            for h in range(2):
                for j in halves(q):
                    add((k, h, d, s, j), ry[k, m, h, j])
            y_copy(k, m + 4, q).start()

    def y_finish(k, q=None):
        for m in (2, 3, 4, 5):
            y_copy(k, m, q).wait_recv()
        for h in range(2):
            for s, (m, n) in enumerate(((3, 4), (2, 5))):
                for j in halves(q):
                    add((k, h, y, s, j), ry[k, m, h, j], ry[k, n, h, j])
        yx_copy(k, q).start()

    def x_middle(k, q=None):
        v = k - SPLIT
        x_copy(k, q).wait_recv()
        for d in (yo, yr, yl, y):
            for s in range(2):
                for j in halves(q):
                    add((k, xh, d, s, j), rx[v, d, s, j])
            if d is yo:
                xy_copy(k, 0, q).start()
                xy_copy(k, 1, q).start()
        xy_copy(k, 2, q).start()
        xy_copy(k, 3, q).start()

    def xy_middle(k, q=None):
        v = k - SPLIT
        for m, d, s in ((0, yr, 0), (1, yl, 1)):
            xy_copy(k, m, q).wait_recv()
            for j in halves(q):
                add((k, xh, d, s, j), rxy[v, m, j])
            xy_copy(k, m + 4, q).start()

    @pl.loop(0, SPLIT)
    def _(k):
        y_middle(k)

    y_middle(SPLIT, 0)
    x_middle(SPLIT + 1)

    def agrad(q, tok):
        wide = jnp.concatenate(
            [
                w5[(q // 4) * 2 + k // 4, k % 4, lax.rem(q, 4), h * 256 : h * 256 + 256]
                for k in range(8)
                for h in range(2)
            ],
            axis=1,
        )
        rows = jnp.concatenate([hg[k, tok, :] for k in range(8)], axis=1)
        return lax.dot_general(rows, wide, (((1,), (1,)), ((), ())), preferred_element_type=F32)

    ags = av.at[0:TOK]

    @pl.loop(0, 8)
    def _(i):
        ags[:, pl.ds(pl.multiple_of(i * 256, 256), 256)] = agrad(i, theirs).astype(BF)

    ag_copy = remote(ags, ag_out, ag_send, ag_recv, sibling)
    ag_copy.start()
    ag_copy.wait_recv()

    @pl.loop(0, 8)
    def _(i):
        col = pl.ds(pl.multiple_of(i * 256, 256), 256)
        ag_out[:, col] = (agrad(i, mine) + ag_out[:, col].astype(F32)).astype(BF)

    x_middle(SPLIT + 2)
    y_finish(0)
    y_finish(1)
    x_middle(SPLIT + 3)
    xy_middle(SPLIT + 1)
    y_finish(2)
    y_finish(3)
    y_finish(SPLIT, 0)
    xy_middle(SPLIT + 2)
    x_middle(SPLIT, 1)
    xy_middle(SPLIT + 3)
    xy_middle(SPLIT, 1)

    def fin(k, s):
        return av.at[pl.ds(pl.multiple_of(TOK + s * 128, 128), 128), pl.ds(pl.multiple_of(k * 256, 256), 256)]

    def block_columns(k):
        return pl.ds(pl.multiple_of(k * 512 + c * 256, 256), 256)

    def fin_copy(k):
        return remote(
            fin(k, other), wg_out.at[:, block_columns(k)], fin_send.at[k], fin_recv.at[k], sibling
        )

    def y_total(k, j):
        return part[k, xh, y, :, j].astype(F32) + ryx[k, :, j].astype(F32)

    def x_total(k, j):
        v = k - SPLIT
        rows = [
            part[k, xh, y, s, j].astype(F32) + rxy[v, m, j].astype(F32) + rxy[v, n, j].astype(F32)
            for s, (m, n) in enumerate(((3, 4), (2, 5)))
        ]
        return jnp.stack(rows)

    def deliver(k, left_half, right_half):
        total = jnp.concatenate([left_half, right_half], axis=2).astype(BF)
        fin(k, 0)[...] = total[0]
        fin(k, 1)[...] = total[1]
        fin_copy(k).start()
        wg_out[:, block_columns(k)] = fin(k, c)[...]

    def x_arrive(k, q=None):
        for m in (2, 3, 4, 5):
            xy_copy(k, m, q).wait_recv()

    @pl.loop(0, SPLIT)
    def _(k):
        yx_copy(k).wait_recv()
        deliver(k, y_total(k, 0), y_total(k, 1))

    @pl.loop(SPLIT + 1, 8)
    def _(k):
        x_arrive(k)
        deliver(k, x_total(k, 0), x_total(k, 1))

    yx_copy(SPLIT, 0).wait_recv()
    x_arrive(SPLIT, 1)
    deliver(SPLIT, y_total(SPLIT, 0), x_total(SPLIT, 1))

    @pl.loop(0, 8)
    def _(k):
        a, b = hgo_copies(k)
        a.wait()
        for copy in (b, fin_copy(k)):
            copy.wait_recv()
            copy.wait_send()

    def y_drain(k, q=None):
        for m in range(6):
            y_copy(k, m, q).wait_send()
        yx_copy(k, q).wait_send()

    def x_drain(k, q=None):
        x_copy(k, q).wait_send()
        for m in range(6):
            xy_copy(k, m, q).wait_send()

    @pl.loop(0, SPLIT)
    def _(k):
        y_drain(k)

    @pl.loop(SPLIT + 1, 8)
    def _(k):
        x_drain(k)

    y_drain(SPLIT, 0)
    x_drain(SPLIT, 1)

    ag_copy.wait_send()
    for copy in norm_copies + factor_copies + gather_copies + [attn_send]:
        copy.wait_send()
    for _, sent_old in old_pairs:
        sent_old.wait_send()
    for copy in new_copies:
        copy.wait()
    for _, b in act_copies:
        b.wait_send()


def hand_over(*refs):
    sems = refs[10]
    copies = [pltpu.make_async_copy(refs[i], refs[5 + i], sems.at[i]) for i in range(5)]
    for copy in copies:
        copy.start()
    for copy in copies:
        copy.wait()


def shards(local_params, params, momentum, old_mask, attn, resid, gain, out_grad):
    hbm = pl.BlockSpec(memory_space=pl.ANY)
    vmem = pl.BlockSpec(memory_space=pltpu.VMEM)
    smem = pl.BlockSpec(memory_space=pltpu.SMEM)
    dma = pltpu.SemaphoreType.DMA
    par, mom, wg, ag, hg = pl.pallas_call(
        kernel,
        out_shape=(
            pltpu.VMEM((128, 512), F32),
            pltpu.VMEM((128, 512), F32),
            pltpu.VMEM((128, D), BF),
            pltpu.VMEM((TOK, HQ), BF),
            pltpu.VMEM((TOK, D), BF),
        ),
        in_specs=[hbm, hbm, hbm, smem, hbm, hbm, vmem, hbm],
        out_specs=(vmem,) * 5,
        scratch_shapes=[
            pltpu.VMEM((128, 512), F32),
            pltpu.VMEM((128, 512), F32),
            pltpu.VMEM((8, 128), F32),
            pltpu.VMEM((16, 8, 128), F32),
            pltpu.VMEM((8, 128), F32),
            pltpu.VMEM((8, 8, 128), F32),
            pltpu.VMEM((4, 4, 4, 512, 128), BF),
            pltpu.VMEM((1024, 2048), BF),
            pltpu.VMEM((8, 1024, 256), BF),
            pltpu.VMEM((8, 1024, 256), BF),
            pltpu.VMEM((8, 1024, 256), F32),
            pltpu.VMEM((8, 256, 1024), BF),
            pltpu.VMEM((2, 1024, 128), F32),
            pltpu.VMEM((1024, 128), F32),
            pltpu.VMEM((8, 2, 4, 2, 2, 128, 128), BF),
            pltpu.VMEM((SPLIT + 1, 6, 2, 2, 128, 128), BF),
            pltpu.VMEM((SPLIT + 1, 2, 2, 128, 128), BF),
            pltpu.VMEM((8 - SPLIT, 4, 2, 2, 128, 128), BF),
            pltpu.VMEM((8 - SPLIT, 6, 2, 128, 128), BF),
            dma((4, 8)), dma((2,)), dma((2,)), dma((2,)), dma((2,)), dma((2,)),
            dma((16,)), dma((16,)), dma((16,)), dma((16,)), dma((8,)), dma((8,)),
            dma((17,)), dma((17,)), dma((17,)), dma((108,)), dma((108,)), dma((4,)), dma((4,)),
            dma((SPLIT + 1, 6)), dma((SPLIT + 1, 6)), dma((SPLIT + 1,)), dma((SPLIT + 1,)),
            dma((8 - SPLIT,)), dma((8 - SPLIT,)), dma((8 - SPLIT, 6)), dma((8 - SPLIT, 6)),
            dma((8,)), dma((8,)), dma, dma, dma((8,)), dma((8,)), dma((8,)),
        ],
        compiler_params=pltpu.CompilerParams(
            collective_id=0, has_side_effects=True, vmem_limit_bytes=54 << 20
        ),
        cost_estimate=pl.CostEstimate(flops=26 * 10**9, bytes_accessed=40 * 2**20, transcendentals=0),
        name="outer_inner",
    )(local_params[0], params, momentum, old_mask, attn[0], resid[0], gain, out_grad[0])
    par, mom, wg, ag, hg = pl.pallas_call(
        hand_over,
        out_shape=tuple(jax.ShapeDtypeStruct(v.shape, v.dtype) for v in (par, mom, wg, ag, hg)),
        in_specs=[vmem] * 5,
        out_specs=(hbm,) * 5,
        scratch_shapes=[dma((5,))],
        compiler_params=pltpu.CompilerParams(vmem_limit_bytes=1 << 20),
        name="hand_over",
    )(*(pltpu.with_memory_space_constraint(v, pltpu.VMEM) for v in (par, mom, wg, ag, hg)))
    return (par, mom, wg[None], ag[None], hg[None])


def solution(mesh):
    return jax.shard_map(
        shards,
        mesh=mesh,
        in_specs=(
            P("replica", "fsdp", None),
            P("fsdp", None),
            P("fsdp", None),
            P(),
            P("replica", "fsdp", None),
            P("replica", "fsdp", None),
            P(),
            P("replica", "fsdp", None),
        ),
        out_specs=(
            P("fsdp", "replica"),
            P("fsdp", "replica"),
            P("replica", "fsdp", None),
            P("replica", "fsdp", None),
            P("replica", "fsdp", None),
        ),
        check_vma=False,
    )
```
